256 devices in a mesh: row: 16 (over z_hi, x), col: 16 (over z_lo, y, core).
Axes of the slice: x: 4, y: 4, z: 8 (z_hi: 4, z_lo: 2; z = z_hi * 2 + z_lo), core: 2. Of those that a mesh axis runs over, the one named last changes fastest.
Arguments:
- values: bfloat16 [16, 16, 2, 18, 128, 128], P('row', 'col'), may hold values from -6 to 6
- mask_x: int32 [16, 16, 2, 18], P('row', 'col'), may hold values from 0 to 1, as said below
- mask_sq: int32 [16, 16, 2, 26], P('row', 'col'), may hold values from 0 to 1, as said below
Outputs:
- result: bfloat16 [16, 16, 2, 18, 128, 128], P('row', 'col')
The draws below stay inside these ranges and needn't reach their ends.
Inputs may be any that keep to these rules, and one draw needn't show every extreme that they name: `mask_x`: in every row the slot of offset (0, 0) and the row's own layer is 1, and at least one row has all 18 slots equal to 1. `mask_sq`: 1 wherever mask_x is 1 in the slot with the same offset and layer.
All inputs are finite; a program needn't handle non-finite values.
Results may differ from the reference program's by a relative error of at most 0.0033.
Values may be sent and summed in bfloat16 or wider, within the bound.
A program may use at most 64 MiB of HBM per device.

```python
import jax
import jax.numpy as jnp
import numpy as np
from jax import lax

BS = 128
LAYERS = 2
KB = 18
KSQ = 26
AA = 16
BB = 16


given_offsets = [(u, v) for u in (-1, 0, 1) for v in (-1, 0, 1)]


square_offsets = [(u, v) for u in range(-2, 3) for v in range(-2, 3) if u * u + v * v <= 4]


def shared_mask(key):
    key = jax.random.fold_in(key, 101)
    level_key, toss_key, row_key = jax.random.split(key, 3)
    density = jax.random.randint(level_key, (AA, BB, LAYERS, 1), 1, 11)
    tosses = jax.random.randint(toss_key, (AA, BB, LAYERS, KB), 0, 10)
    layer_index = jnp.arange(LAYERS, dtype=jnp.int32)[None, None, :, None]
    slot_index = jnp.arange(KB, dtype=jnp.int32)[None, None, None, :]
    diagonal = slot_index == 4 * LAYERS + layer_index
    site_number = (jnp.arange(AA, dtype=jnp.int32)[:, None, None] * BB + jnp.arange(BB, dtype=jnp.int32)[None, :, None]) * LAYERS + jnp.arange(LAYERS, dtype=jnp.int32)[None, None, :]
    chosen = jax.random.randint(row_key, (), 0, AA * BB * LAYERS)
    full_row = (site_number == chosen)[..., None]
    return (tosses < density) | diagonal | full_row


def draw_mask_x(key, part):
    return shared_mask(key).astype(jnp.int32)


def draw_mask_sq(key, part):
    inside = shared_mask(key)
    key = jax.random.fold_in(key, 7)
    extra = jax.random.randint(key, (AA, BB, LAYERS, KSQ), 0, 2) > 0
    source = []
    for offset in square_offsets:
        for m in range(LAYERS):
            if offset in given_offsets:
                source.append(given_offsets.index(offset) * LAYERS + m)
            else:
                source.append(-1)
    source = np.array(source, dtype=np.int32)
    carried = jnp.take(inside, np.maximum(source, 0), axis=3) & (source >= 0)[None, None, None, :]
    return (carried | extra).astype(jnp.int32)


def block_scale(rng, extent, cuts, smallest, top_value):
    gain, own = 1.0, jax.random.fold_in(rng, 6)
    for axis_at, parts in cuts:
        draws = jnp.exp(jax.random.uniform(jax.random.fold_in(own, axis_at), (parts,), jnp.float32, smallest / len(cuts), top_value / len(cuts)))
        gain = gain * jnp.repeat(draws, extent[axis_at] // parts).reshape([-1 if axis == axis_at else 1 for axis in range(len(extent))])
    return gain


def scatter_about(rng, shape, scale, bound, shards=(), held_as=jnp.bfloat16):
    values = scale * jax.random.normal(rng, shape, jnp.float32)
    if shards:
        values = values * block_scale(rng, shape, shards, -0.22, 0.18)
    return jnp.clip(values, -bound, bound).astype(held_as)


def setup_inputs(seed: int = 0) -> dict:
    streams_of = jax.random.split(jax.random.key(seed), 4)
    return {
        "values": scatter_about(streams_of[0], (AA, BB, LAYERS, KB, BS, BS), 1.0, 6.0, ((0, 16), (1, 16))),
        "mask_x": draw_mask_x(jax.random.fold_in(streams_of[3], 71), 0),
        "mask_sq": draw_mask_sq(jax.random.fold_in(streams_of[3], 71), 0),
    }


given_offsets = [(u, v) for u in (-1, 0, 1) for v in (-1, 0, 1)]
square_offsets = [(u, v) for u in range(-2, 3) for v in range(-2, 3) if u * u + v * v <= 4]


def combine(left_blocks, neighbour_rows, out_offsets, left_offsets, right_offsets, layers):
    outputs = []
    for target in out_offsets:
        pair_list = []
        for position, (p, q) in enumerate(left_offsets):
            remainder = (target[0] - p, target[1] - q)
            if remainder in right_offsets:
                pair_list.append((position, p, q, right_offsets.index(remainder)))
        left_slots = np.array([e[0] * layers + k for e in pair_list for k in range(layers)], dtype=np.int32)
        picked = jnp.take(left_blocks, left_slots, axis=3).astype(jnp.float32)
        partner = jnp.concatenate([neighbour_rows(e[1], e[2], [e[3] * layers + m for m in range(layers)]) for e in pair_list], axis=2).astype(jnp.float32)
        outputs.append(jnp.einsum("abikxy,abkmyz->abimxz", picked, partner))
    stacked = jnp.stack(outputs, axis=3)
    stacked_shape = stacked.shape
    return stacked.reshape(stacked_shape[0], stacked_shape[1], stacked_shape[2], stacked_shape[3] * stacked_shape[4], stacked_shape[5], stacked_shape[6])


def shifted_rows(field, a, s):
    return lax.dynamic_index_in_dim(field, (a + s) % field.shape[0], 0, keepdims=True)


def reference(values, mask_x, mask_sq):
    layers = values.shape[2]
    masked = jnp.where(mask_x[..., None, None] > 0, values, jnp.zeros_like(values))

    def square_row(a):
        nearby = {s: shifted_rows(masked, a, s) for s in (-1, 0, 1)}

        def given_rows(s, t, slots):
            return jnp.roll(jnp.take(nearby[s], np.array(slots, dtype=np.int32), axis=3), -t, axis=1)

        square = combine(nearby[0], given_rows, square_offsets, given_offsets, given_offsets, layers)
        keep_mask = shifted_rows(mask_sq, a, 0)
        kept = jnp.where(keep_mask[..., None, None] > 0, square * (0.25 / BS), jnp.float32(0.0))
        return kept.astype(jnp.bfloat16)[0]

    filtered = lax.map(square_row, jnp.arange(AA, dtype=jnp.int32))

    def cube_row(a):
        nearby = {s: shifted_rows(filtered, a, s) for s in (-1, 0, 1)}

        def square_rows(s, t, slots):
            return jnp.roll(jnp.take(nearby[s], np.array(slots, dtype=np.int32), axis=3), -t, axis=1)

        own_blocks = shifted_rows(masked, a, 0)
        cube_part = combine(own_blocks, square_rows, given_offsets, given_offsets, square_offsets, layers)
        keep_mask = shifted_rows(mask_x, a, 0)
        updated = jnp.where(keep_mask[..., None, None] > 0, 1.5 * own_blocks.astype(jnp.float32) - 0.5 * cube_part, jnp.float32(0.0))
        return updated.astype(jnp.bfloat16)[0]

    return lax.map(cube_row, jnp.arange(AA, dtype=jnp.int32))
```

```python
import jax
import jax.numpy as jnp
from jax import lax
from jax.experimental import pallas as pl
from jax.experimental.pallas import tpu as pltpu
from jax.sharding import PartitionSpec as P

BS = 128
UNIT = 2 * BS
MESH = pl.DeviceIdType.MESH

square_units = [(0, -2), (0, 2)] + [(u, 0) for u in range(-2, 3)]
square_units += [(u, -1) for u in (-1, 0, 1)] + [(u, 1) for u in (-1, 0, 1)]
square_at = {t: n for n, t in enumerate(square_units)}
square_slots = [(u, v) for u in range(-2, 3) for v in range(-2, 3) if u * u + v * v <= 4]

left_square = [(u, 0) for u in range(-2, 3)] + [(0, 2)] + [(u, 1) for u in (-1, 0, 1)]
right_square = [(u, 0) for u in range(-2, 3)] + [(0, -2)] + [(u, -1) for u in (-1, 0, 1)]
left_cube = [(u, v) for v in (-1, 1, 0) for u in (-1, 0, 1)]
right_cube = [(u, v) for v in (1, -1, 0) for u in (-1, 0, 1)]


def given_at(u, v):
    return (v + 1) * 3 + u + 1


def make_kernel(rows, cols):
    def kernel(
        values, mask_x, mask_sq, out,
        staged, own, above, below, from_left, from_right,
        give_left, give_right, got_left, got_right,
        filtered, filt_above, filt_below,
        give_left2, give_right2, got_left2, got_right2,
        acc, result, load_sem, out_sem, send_sem, recv_sem,
    ):
        a, b = lax.axis_index("row"), lax.axis_index("col")
        up = (lax.rem(a + rows - 1, rows), b)
        down = (lax.rem(a + 1, rows), b)
        left = (a, lax.rem(b + cols - 1, cols))
        right = (a, lax.rem(b + 1, cols))

        loads = {}
        for c in (0, 2, 1):
            loads[c] = pltpu.make_async_copy(values.at[:, :, c], staged.at[c], load_sem.at[c])
            loads[c].start()

        barrier = pltpu.get_barrier_semaphore()
        for device in (up, down, left, right):
            pl.semaphore_signal(barrier, inc=1, device_id=device, device_id_type=MESH)
        pl.semaphore_wait(barrier, 4)

        sent = []

        def send(src, dst, device):
            n = len(sent)
            copy = pltpu.make_async_remote_copy(
                src_ref=src, dst_ref=dst, send_sem=send_sem.at[n], recv_sem=recv_sem.at[n],
                device_id=device, device_id_type=MESH,
            )
            copy.start()
            sent.append(copy)
            return copy

        def blocks(ref, unit):
            for l in range(2):
                for m in range(2):
                    yield l, m, ref.at[unit, pl.ds(l * BS, BS), pl.ds(m * BS, BS)]

        vertical = {}
        for c in (0, 2, 1):
            loads[c].wait()
            for ui in range(3):
                for l, m, block in blocks(own, c * 3 + ui):
                    keep = mask_x[0, 0, l, (ui * 3 + c) * 2 + m] > 0
                    value = staged[c, l, ui, m]
                    block[...] = jnp.where(keep, value, jnp.zeros_like(value))
            span = pl.ds(c * 3, 3)
            vertical[c] = (
                send(own.at[span], below.at[span], up),
                send(own.at[span], above.at[span], down),
            )
            if c == 0:
                to_left = send(own.at[span], from_right, left)
            if c == 2:
                to_right = send(own.at[span], from_left, right)

        row_of = {-1: above, 0: own, 1: below}
        filt_of = {
            -1: (filt_above, lambda u, v: down_units.index((u, v))),
            0: (filtered, lambda u, v: square_at[(u, v)]),
            1: (filt_below, lambda u, v: up_units.index((u, v))),
        }
        factor = {
            1: lambda p: from_left[p + 1],
            -1: lambda p: from_right[p + 1],
            0: lambda p: own[given_at(p, 0)],
        }

        def product_square(q, t):
            total = None
            for p in (-1, 0, 1):
                u, v = t[0] - p, t[1] - q
                if abs(u) <= 1 and abs(v) <= 1:
                    term = jnp.dot(
                        factor[q](p), row_of[p][given_at(u, v)], preferred_element_type=jnp.float32
                    )
                    total = term if total is None else total + term
            return total

        def product_cube(q, t):
            total = None
            for p in (-1, 0, 1):
                u, v = t[0] - p, t[1] - q
                if u * u + v * v <= 4:
                    ref, place = filt_of[p]
                    term = jnp.dot(factor[q](p), ref[place(u, v)], preferred_element_type=jnp.float32)
                    total = term if total is None else total + term
            return total

        def give(product, q, order, targets, buffer, landing, device):
            first = order.index(targets[0])
            for n, t in enumerate(targets):
                buffer[first + n] = product(q, t).astype(jnp.bfloat16)
            span = pl.ds(first, len(targets))
            return send(buffer.at[span], landing.at[span], device)

        def give_left_square(targets):
            return give(product_square, 1, left_square, targets, give_left, got_right, left)

        def give_right_square(targets):
            return give(product_square, -1, right_square, targets, give_right, got_left, right)

        def finish_square(t, total):
            s = square_at[t]
            if t in left_square:
                part = got_right[left_square.index(t)].astype(jnp.float32)
                total = part if total is None else total + part
            if t in right_square:
                part = got_left[right_square.index(t)].astype(jnp.float32)
                total = part if total is None else total + part
            total = total * (0.25 / BS)
            for l, m, block in blocks(filtered, s):
                keep = mask_sq[0, 0, l, square_slots.index(t) * 2 + m] > 0
                value = total[l * BS : (l + 1) * BS, m * BS : (m + 1) * BS]
                block[...] = jnp.where(keep, value, jnp.zeros_like(value)).astype(jnp.bfloat16)

        up_units = [(0, -2), (0, 2)] + [(u, 0) for u in (-2, -1, 0)]
        up_units += [(u, v) for v in (-1, 1) for u in (-1, 0)]
        down_units = [(0, -2), (0, 2)] + [(u, 0) for u in (0, 1, 2)]
        down_units += [(u, v) for v in (-1, 1) for u in (0, 1)]

        def send_filtered(units_up, units_down):
            copies = []
            for units, order, landing, device in (
                (units_up, up_units, filt_below, up),
                (units_down, down_units, filt_above, down),
            ):
                copies.append(
                    send(
                        filtered.at[pl.ds(square_at[units[0]], len(units))],
                        landing.at[pl.ds(order.index(units[0]), len(units))],
                        device,
                    )
                )
            return copies

        def await_recv(*copies):
            for copy in copies:
                copy.wait_recv()

        await_recv(to_left, to_right)
        await_recv(*vertical[0])
        r_far = give_right_square([(0, -2)])
        l_mid = give_left_square([(u, 0) for u in range(-2, 3)])
        await_recv(r_far)
        finish_square((0, -2), None)
        f_left = send_filtered([(0, -2)], [(0, -2)])
        await_recv(*vertical[2])
        l_far = give_left_square([(0, 2)])
        r_mid = give_right_square([(u, 0) for u in range(-2, 3)])
        await_recv(l_far)
        finish_square((0, 2), None)
        f_right = send_filtered([(0, 2)], [(0, 2)])
        for n, v in enumerate((-1, 1)):
            for u in (-1, 0, 1):
                acc[n * 3 + u + 1] = product_square(0, (u, v))
        await_recv(*vertical[1])
        near = []
        for u in (0, -1, 1):
            near.append(give_left_square([(u, 1)]))
            near.append(give_right_square([(u, -1)]))
        await_recv(l_mid, r_mid)
        for u in range(-2, 3):
            finish_square((u, 0), product_square(0, (u, 0)))
        f_mid = send_filtered([(u, 0) for u in (-2, -1, 0)], [(u, 0) for u in (0, 1, 2)])
        await_recv(*near)
        f_near = []
        for n, v in enumerate((-1, 1)):
            for u in (-1, 0, 1):
                finish_square((u, v), acc[n * 3 + u + 1])
            f_near.append(send_filtered([(u, v) for u in (-1, 0)], [(u, v) for u in (0, 1)]))

        def give_left_cube(v):
            return give(
                product_cube, 1, left_cube, [(u, v) for u in (-1, 0, 1)], give_left2, got_right2, left
            )

        def give_right_cube(v):
            return give(
                product_cube, -1, right_cube, [(u, v) for u in (-1, 0, 1)], give_right2, got_left2, right
            )

        def finish_cube(t, total):
            u, v = t
            total = total + got_right2[left_cube.index(t)].astype(jnp.float32)
            total = total + got_left2[right_cube.index(t)].astype(jnp.float32)
            total = 1.5 * own[given_at(u, v)].astype(jnp.float32) - 0.5 * total
            for l in range(2):
                for m in range(2):
                    keep = mask_x[0, 0, l, ((u + 1) * 3 + v + 1) * 2 + m] > 0
                    value = total[l * BS : (l + 1) * BS, m * BS : (m + 1) * BS]
                    result[v + 1, l, u + 1, m] = jnp.where(keep, value, jnp.zeros_like(value)).astype(
                        jnp.bfloat16
                    )

        stores = []

        def store(v):
            copy = pltpu.make_async_copy(result.at[v + 1], out.at[:, :, v + 1], out_sem.at[v + 1])
            copy.start()
            stores.append(copy)

        await_recv(*f_left)
        c_l = [give_left_cube(-1)]
        await_recv(*f_right)
        c_r = [give_right_cube(1)]
        await_recv(*f_mid)
        c_l.append(give_left_cube(1))
        c_r.append(give_right_cube(-1))
        for u in (-1, 0, 1):
            acc[6 + u + 1] = product_cube(0, (u, 0))
        await_recv(*f_near[0])
        c_l.append(give_left_cube(0))
        await_recv(*f_near[1])
        c_r.append(give_right_cube(0))
        await_recv(c_l[0], c_l[1], c_r[0], c_r[1])
        for v in (-1, 1):
            for u in (-1, 0, 1):
                finish_cube((u, v), product_cube(0, (u, v)))
            store(v)
        await_recv(c_l[2], c_r[2])
        for u in (-1, 0, 1):
            finish_cube((u, 0), acc[6 + u + 1])
        store(0)
        for copy in sent:
            copy.wait_send()
        for copy in stores:
            copy.wait()

    return kernel


def solution(mesh):
    rows, cols = mesh.shape["row"], mesh.shape["col"]

    def units(n, dtype=jnp.bfloat16):
        return pltpu.VMEM((n, UNIT, UNIT), dtype)

    def local(values, mask_x, mask_sq):
        grid = values.reshape(2, 3, 3, 2, BS, BS)
        out = pl.pallas_call(
            make_kernel(rows, cols),
            out_shape=jax.ShapeDtypeStruct(grid.shape, jnp.bfloat16),
            in_specs=[
                pl.BlockSpec(memory_space=pl.ANY),
                pl.BlockSpec(memory_space=pltpu.SMEM),
                pl.BlockSpec(memory_space=pltpu.SMEM),
            ],
            out_specs=pl.BlockSpec(memory_space=pl.ANY),
            scratch_shapes=[
                pltpu.VMEM((3, 2, 3, 2, BS, BS), jnp.bfloat16),
                units(9), units(9), units(9), units(3), units(3),
                units(9), units(9), units(9), units(9),
                units(13), units(9), units(9),
                units(9), units(9), units(9), units(9),
                units(9, jnp.float32),
                pltpu.VMEM((3, 2, 3, 2, BS, BS), jnp.bfloat16),
                pltpu.SemaphoreType.DMA((3,)),
                pltpu.SemaphoreType.DMA((3,)),
                pltpu.SemaphoreType.DMA((40,)),
                pltpu.SemaphoreType.DMA((40,)),
            ],
            compiler_params=pltpu.CompilerParams(
                collective_id=0, has_side_effects=True, vmem_limit_bytes=48 * 2**20
            ),
        )(grid, mask_x, mask_sq)
        return out.reshape(values.shape)

    return jax.shard_map(
        local,
        mesh=mesh,
        in_specs=(
            P("row", "col", None, None, None, None),
            P("row", "col", None, None),
            P("row", "col", None, None),
        ),
        out_specs=P("row", "col", None, None, None, None),
        check_vma=False,
    )
```

```python
import jax
import jax.numpy as jnp
from jax import lax
from jax.experimental import pallas as pl
from jax.experimental.pallas import tpu as pltpu
from jax.sharding import PartitionSpec as P

BS = 128
UNIT = 2 * BS
MESH = pl.DeviceIdType.MESH
X = 4

square_units = [(0, -2), (0, 2)] + [(u, 0) for u in range(-2, 3)]
square_units += [(u, -1) for u in (-1, 0, 1)] + [(u, 1) for u in (-1, 0, 1)]
up_units = [(0, -2), (0, 2)] + [(u, 0) for u in (-2, -1, 0)]
up_units += [(u, v) for v in (-1, 1) for u in (-1, 0)]
down_units = [(0, -2), (0, 2)] + [(u, 0) for u in (0, 1, 2)]
down_units += [(u, v) for v in (-1, 1) for u in (0, 1)]
square_slots = [(u, v) for u in range(-2, 3) for v in range(-2, 3) if u * u + v * v <= 4]

left_square = [(u, 0) for u in range(-2, 3)] + [(0, 2)] + [(u, 1) for u in (-1, 0, 1)]
right_square = [(u, 0) for u in range(-2, 3)] + [(0, -2)] + [(u, -1) for u in (-1, 0, 1)]
left_cube = [(u, v) for v in (-1, 1, 0) for u in (-1, 0, 1)]
right_cube = [(u, v) for v in (1, -1, 0) for u in (-1, 0, 1)]


def given_at(u, v):
    return (v + 1) * 3 + u + 1


def unit(n, count=1):
    return pl.ds(n * UNIT, count * UNIT)


def make_kernel(rows, cols):
    def kernel(
        values, mask_x, mask_sq, out,
        staged, own, above, below, from_left, from_right,
        give_left, give_right, got_left, got_right,
        filtered, filt_above, filt_below,
        give_left2, give_right2, got_left2, got_right2,
        passing, acc, result, load_sem, out_sem, send_sem, recv_sem, pass_recv_sem, pass_send_sem,
    ):
        a, b = lax.axis_index("row"), lax.axis_index("col")

        def row(shift):
            return (lax.rem(a + shift + rows, rows), b)

        up, down = row(-1), row(1)
        left = (a, lax.rem(b + cols - 1, cols))
        right = (a, lax.rem(b + 1, cols))
        x = lax.rem(a, X)
        first, last = x == 0, x == X - 1

        loads = {}
        for c in (0, 2, 1):
            loads[c] = pltpu.make_async_copy(values.at[:, :, c], staged.at[c], load_sem.at[c])
            loads[c].start()

        barrier = pltpu.get_barrier_semaphore()

        def greet(device):
            pl.semaphore_signal(barrier, inc=1, device_id=device, device_id_type=MESH)

        for device in (up, down, left, right):
            greet(device)

        @pl.when(first)
        def _():
            greet(row(X - 1))
            greet(row(-X))

        @pl.when(last)
        def _():
            greet(row(1 - X))
            greet(row(X))

        pl.semaphore_wait(barrier, jnp.where(first | last, 6, 4))

        sent = []

        def make(src, dst, device):
            n = len(sent)
            copy = pltpu.make_async_remote_copy(
                src_ref=src, dst_ref=dst, send_sem=send_sem.at[n], recv_sem=recv_sem.at[n],
                device_id=device, device_id_type=MESH,
            )
            sent.append(copy)
            return copy

        def send(src, dst, device):
            copy = make(src, dst, device)
            copy.start()
            return [copy]

        passed = []

        def send_rows(src, src_unit, dst, dst_unit, count, goes_up, base):
            device, at_wrap, partner = (up, first, row(X - 1)) if goes_up else (down, last, row(1 - X))
            half = count * UNIT // 2
            straight = make(
                src.at[pl.ds(src_unit * UNIT, half)], dst.at[pl.ds(dst_unit * UNIT, half)], device
            )
            n = len(passed) // 2
            src_half = src.at[pl.ds(src_unit * UNIT + half, half)]
            dst_half = dst.at[pl.ds(dst_unit * UNIT + half, half)]
            hold = passing.at[pl.ds((base + dst_unit) * UNIT + half, half)]
            other = make(src_half, dst_half, device)
            k = len(sent) - 1
            detour = pltpu.make_async_remote_copy(
                src_ref=src_half, dst_ref=hold, send_sem=send_sem.at[k],
                recv_sem=pass_recv_sem.at[n], device_id=partner, device_id_type=MESH,
            )
            onward = pltpu.make_async_remote_copy(
                src_ref=hold, dst_ref=dst_half, send_sem=pass_send_sem.at[n],
                recv_sem=recv_sem.at[k], device_id=row(-X if goes_up else X), device_id_type=MESH,
            )
            passed.append((last if goes_up else first, detour, onward))
            straight.start()

            @pl.when(at_wrap)
            def _():
                detour.start()

            @pl.when(jnp.logical_not(at_wrap))
            def _():
                other.start()

            return [straight, other]

        handed = [0]

        def pass_on():
            for condition, detour, onward in passed[handed[0] : handed[0] + 2]:

                @pl.when(condition)
                def _():
                    detour.wait_recv()
                    onward.start()

            handed[0] += 2

        def blocks(ref, n):
            for l in range(2):
                for m in range(2):
                    yield l, m, ref.at[pl.ds(n * UNIT + l * BS, BS), pl.ds(m * BS, BS)]

        vertical = {}
        for c in (0, 2, 1):
            loads[c].wait()
            for ui in range(3):
                for l, m, block in blocks(own, c * 3 + ui):
                    keep = mask_x[0, 0, l, (ui * 3 + c) * 2 + m] > 0
                    value = staged[c, l, ui, m]
                    block[...] = jnp.where(keep, value, jnp.zeros_like(value))
            vertical[c] = send_rows(own, c * 3, below, c * 3, 3, True, 0)
            vertical[c] += send_rows(own, c * 3, above, c * 3, 3, False, 0)
            if c == 0:
                to_left = send(own.at[unit(c * 3, 3)], from_right, left)
            if c == 2:
                to_right = send(own.at[unit(c * 3, 3)], from_left, right)

        row_of = {-1: above, 0: own, 1: below}
        filt_of = {
            -1: (filt_above, down_units), 0: (filtered, square_units), 1: (filt_below, up_units)
        }
        factor = {
            1: lambda p: from_left[unit(p + 1)],
            -1: lambda p: from_right[unit(p + 1)],
            0: lambda p: own[unit(given_at(p, 0))],
        }

        def product_square(q, t):
            total = None
            for p in (-1, 0, 1):
                u, v = t[0] - p, t[1] - q
                if abs(u) <= 1 and abs(v) <= 1:
                    term = jnp.dot(
                        factor[q](p), row_of[p][unit(given_at(u, v))],
                        preferred_element_type=jnp.float32,
                    )
                    total = term if total is None else total + term
            return total

        def product_cube(q, t):
            total = None
            for p in (-1, 0, 1):
                u, v = t[0] - p, t[1] - q
                if u * u + v * v <= 4:
                    ref, order = filt_of[p]
                    term = jnp.dot(
                        factor[q](p), ref[unit(order.index((u, v)))],
                        preferred_element_type=jnp.float32,
                    )
                    total = term if total is None else total + term
            return total

        def give(product, q, order, targets, buffer, landing, device):
            at = order.index(targets[0])
            for n, t in enumerate(targets):
                buffer[unit(at + n)] = product(q, t).astype(jnp.bfloat16)
            span = unit(at, len(targets))
            return send(buffer.at[span], landing.at[span], device)

        def give_left_square(targets):
            return give(product_square, 1, left_square, targets, give_left, got_right, left)

        def give_right_square(targets):
            return give(product_square, -1, right_square, targets, give_right, got_left, right)

        def finish_square(t, total):
            if t in left_square:
                part = got_right[unit(left_square.index(t))].astype(jnp.float32)
                total = part if total is None else total + part
            if t in right_square:
                part = got_left[unit(right_square.index(t))].astype(jnp.float32)
                total = part if total is None else total + part
            total = total * (0.25 / BS)
            for l, m, block in blocks(filtered, square_units.index(t)):
                keep = mask_sq[0, 0, l, square_slots.index(t) * 2 + m] > 0
                value = total[l * BS : (l + 1) * BS, m * BS : (m + 1) * BS]
                block[...] = jnp.where(keep, value, jnp.zeros_like(value)).astype(jnp.bfloat16)

        def send_filtered(units_up, units_down):
            copies = []
            for units, order, landing, goes_up in (
                (units_up, up_units, filt_below, True), (units_down, down_units, filt_above, False)
            ):
                copies += send_rows(
                    filtered, square_units.index(units[0]), landing, order.index(units[0]),
                    len(units), goes_up, 9,
                )
            return copies

        def await_recv(*groups):
            for group in groups:
                for copy in group:
                    copy.wait_recv()

        await_recv(to_left, to_right)
        pass_on()
        await_recv(vertical[0])
        r_far = give_right_square([(0, -2)])
        l_mid = give_left_square([(u, 0) for u in range(-2, 3)])
        pass_on()
        await_recv(r_far)
        finish_square((0, -2), None)
        f_left = send_filtered([(0, -2)], [(0, -2)])
        await_recv(vertical[2])
        l_far = give_left_square([(0, 2)])
        r_mid = give_right_square([(u, 0) for u in range(-2, 3)])
        pass_on()
        await_recv(l_far)
        finish_square((0, 2), None)
        f_right = send_filtered([(0, 2)], [(0, 2)])
        for n, v in enumerate((-1, 1)):
            for u in (-1, 0, 1):
                acc[unit(n * 3 + u + 1)] = product_square(0, (u, v))
        await_recv(vertical[1])
        near = []
        for u in (0, -1, 1):
            near += give_left_square([(u, 1)])
            near += give_right_square([(u, -1)])
        pass_on()
        pass_on()
        await_recv(l_mid, r_mid)
        for u in range(-2, 3):
            finish_square((u, 0), product_square(0, (u, 0)))
        f_mid = send_filtered([(u, 0) for u in (-2, -1, 0)], [(u, 0) for u in (0, 1, 2)])
        await_recv(near)
        f_near = []
        for n, v in enumerate((-1, 1)):
            for u in (-1, 0, 1):
                finish_square((u, v), acc[unit(n * 3 + u + 1)])
            f_near.append(send_filtered([(u, v) for u in (-1, 0)], [(u, v) for u in (0, 1)]))

        def give_left_cube(v):
            return give(
                product_cube, 1, left_cube, [(u, v) for u in (-1, 0, 1)], give_left2, got_right2, left
            )

        def give_right_cube(v):
            return give(
                product_cube, -1, right_cube, [(u, v) for u in (-1, 0, 1)], give_right2, got_left2, right
            )

        def finish_cube(t, total):
            u, v = t
            total = total + got_right2[unit(left_cube.index(t))].astype(jnp.float32)
            total = total + got_left2[unit(right_cube.index(t))].astype(jnp.float32)
            total = 1.5 * own[unit(given_at(u, v))].astype(jnp.float32) - 0.5 * total
            for l in range(2):
                for m in range(2):
                    keep = mask_x[0, 0, l, ((u + 1) * 3 + v + 1) * 2 + m] > 0
                    value = total[l * BS : (l + 1) * BS, m * BS : (m + 1) * BS]
                    result[v + 1, l, u + 1, m] = jnp.where(keep, value, jnp.zeros_like(value)).astype(
                        jnp.bfloat16
                    )

        stores = []

        def store(v):
            copy = pltpu.make_async_copy(result.at[v + 1], out.at[:, :, v + 1], out_sem.at[v + 1])
            copy.start()
            stores.append(copy)

        await_recv(f_left)
        c_l = [give_left_cube(-1)]
        await_recv(f_right)
        c_r = [give_right_cube(1)]
        pass_on()
        await_recv(f_mid)
        c_l.append(give_left_cube(1))
        c_r.append(give_right_cube(-1))
        pass_on()
        pass_on()
        for u in (-1, 0, 1):
            acc[unit(6 + u + 1)] = product_cube(0, (u, 0))
        await_recv(f_near[0])
        c_l.append(give_left_cube(0))
        await_recv(f_near[1])
        c_r.append(give_right_cube(0))
        await_recv(c_l[0], c_l[1], c_r[0], c_r[1])
        for v in (-1, 1):
            for u in (-1, 0, 1):
                finish_cube((u, v), product_cube(0, (u, v)))
            store(v)
        await_recv(c_l[2], c_r[2])
        for u in (-1, 0, 1):
            finish_cube((u, 0), acc[unit(6 + u + 1)])
        store(0)
        for copy in sent:
            copy.wait_send()
        for condition, _, onward in passed:

            @pl.when(condition)
            def _():
                onward.wait_send()

        for copy in stores:
            copy.wait()

    return kernel


def solution(mesh):
    rows, cols = mesh.shape["row"], mesh.shape["col"]

    def units(n, dtype=jnp.bfloat16):
        return pltpu.VMEM((n * UNIT, UNIT), dtype)

    def local(values, mask_x, mask_sq):
        grid = values.reshape(2, 3, 3, 2, BS, BS)
        out = pl.pallas_call(
            make_kernel(rows, cols),
            out_shape=jax.ShapeDtypeStruct(grid.shape, jnp.bfloat16),
            in_specs=[
                pl.BlockSpec(memory_space=pl.ANY),
                pl.BlockSpec(memory_space=pltpu.SMEM),
                pl.BlockSpec(memory_space=pltpu.SMEM),
            ],
            out_specs=pl.BlockSpec(memory_space=pl.ANY),
            scratch_shapes=[
                pltpu.VMEM((3, 2, 3, 2, BS, BS), jnp.bfloat16),
                units(9), units(9), units(9), units(3), units(3),
                units(9), units(9), units(9), units(9),
                units(13), units(9), units(9),
                units(9), units(9), units(9), units(9),
                units(18),
                units(9, jnp.float32),
                pltpu.VMEM((3, 2, 3, 2, BS, BS), jnp.bfloat16),
                pltpu.SemaphoreType.DMA((3,)),
                pltpu.SemaphoreType.DMA((3,)),
                pltpu.SemaphoreType.DMA((64,)),
                pltpu.SemaphoreType.DMA((64,)),
                pltpu.SemaphoreType.DMA((16,)),
                pltpu.SemaphoreType.DMA((16,)),
            ],
            compiler_params=pltpu.CompilerParams(
                collective_id=0, has_side_effects=True, vmem_limit_bytes=60 * 2**20
            ),
        )(grid, mask_x, mask_sq)
        return out.reshape(values.shape)

    return jax.shard_map(
        local,
        mesh=mesh,
        in_specs=(
            P("row", "col", None, None, None, None),
            P("row", "col", None, None),
            P("row", "col", None, None),
        ),
        out_specs=P("row", "col", None, None, None, None),
        check_vma=False,
    )
```

```python
import jax
import jax.numpy as jnp
from jax import lax
from jax.experimental import pallas as pl
from jax.experimental.pallas import tpu as pltpu
from jax.sharding import PartitionSpec as P

BS = 128
UNIT = 2 * BS
MESH = pl.DeviceIdType.MESH
X = 4

square_units = [(0, -2), (0, 2)] + [(u, 0) for u in range(-2, 3)]
square_units += [(u, -1) for u in (-1, 0, 1)] + [(u, 1) for u in (-1, 0, 1)]
up_units = [(0, -2), (0, 2)] + [(u, 0) for u in (-2, -1, 0)]
up_units += [(u, v) for v in (-1, 1) for u in (-1, 0)]
down_units = [(0, -2), (0, 2)] + [(u, 0) for u in (0, 1, 2)]
down_units += [(u, v) for v in (-1, 1) for u in (0, 1)]
square_slots = [(u, v) for u in range(-2, 3) for v in range(-2, 3) if u * u + v * v <= 4]

left_square = [(u, 0) for u in range(-2, 3)] + [(0, 2)] + [(u, 1) for u in (-1, 0, 1)]
right_square = [(u, 0) for u in range(-2, 3)] + [(0, -2)] + [(u, -1) for u in (-1, 0, 1)]
left_cube = [(u, v) for v in (-1, 1, 0) for u in (-1, 0, 1)]
right_cube = [(u, v) for v in (1, -1, 0) for u in (-1, 0, 1)]


def given_at(u, v):
    return (v + 1) * 3 + u + 1


def unit(n, count=1):
    return pl.ds(n * UNIT, count * UNIT)


def make_kernel(rows, cols):
    def kernel(
        values, mask_x, mask_sq, out,
        staged, own, above, below, from_left, from_right,
        give_left, give_right, got_left, got_right,
        filtered, filt_above, filt_below,
        give_left2, give_right2, got_left2, got_right2,
        passing, acc, result, load_sem, out_sem, send_sem, recv_sem, pass_recv_sem, pass_send_sem,
    ):
        a, b = lax.axis_index("row"), lax.axis_index("col")

        def row(shift):
            return (lax.rem(a + shift + rows, rows), b)

        up, down = row(-1), row(1)
        left = (a, lax.rem(b + cols - 1, cols))
        right = (a, lax.rem(b + 1, cols))
        x = lax.rem(a, X)
        first, last = x == 0, x == X - 1

        loads = {}
        for c in (0, 2, 1):
            loads[c] = pltpu.make_async_copy(values.at[:, :, c], staged.at[c], load_sem.at[c])
            loads[c].start()

        barrier = pltpu.get_barrier_semaphore()

        def greet(device):
            pl.semaphore_signal(barrier, inc=1, device_id=device, device_id_type=MESH)

        for device in (up, down, left, right):
            greet(device)

        @pl.when(first)
        def _():
            greet(row(X - 1))
            greet(row(-X))

        @pl.when(last)
        def _():
            greet(row(1 - X))
            greet(row(X))

        pl.semaphore_wait(barrier, jnp.where(first | last, 6, 4))

        sent = []

        def make(src, dst, device):
            n = len(sent)
            copy = pltpu.make_async_remote_copy(
                src_ref=src, dst_ref=dst, send_sem=send_sem.at[n], recv_sem=recv_sem.at[n],
                device_id=device, device_id_type=MESH,
            )
            sent.append(copy)
            return copy

        def send(src, dst, device):
            copy = make(src, dst, device)
            copy.start()
            return [copy]

        passed = []

        def send_rows(src, src_unit, dst, dst_unit, count, goes_up, base):
            device, at_wrap, partner = (up, first, row(X - 1)) if goes_up else (down, last, row(1 - X))
            half = count * UNIT // 2
            straight = make(
                src.at[pl.ds(src_unit * UNIT, half)], dst.at[pl.ds(dst_unit * UNIT, half)], device
            )
            n = len(passed) // 2
            src_half = src.at[pl.ds(src_unit * UNIT + half, half)]
            dst_half = dst.at[pl.ds(dst_unit * UNIT + half, half)]
            hold = passing.at[pl.ds((base + dst_unit) * UNIT + half, half)]
            other = make(src_half, dst_half, device)
            k = len(sent) - 1
            detour = pltpu.make_async_remote_copy(
                src_ref=src_half, dst_ref=hold, send_sem=send_sem.at[k],
                recv_sem=pass_recv_sem.at[n], device_id=partner, device_id_type=MESH,
            )
            onward = pltpu.make_async_remote_copy(
                src_ref=hold, dst_ref=dst_half, send_sem=pass_send_sem.at[n],
                recv_sem=recv_sem.at[k], device_id=row(-X if goes_up else X), device_id_type=MESH,
            )
            passed.append((last if goes_up else first, detour, onward))
            straight.start()

            @pl.when(at_wrap)
            def _():
                detour.start()

            @pl.when(jnp.logical_not(at_wrap))
            def _():
                other.start()

            return [straight, other]

        handed = [0]

        def pass_on():
            for condition, detour, onward in passed[handed[0] : handed[0] + 2]:

                @pl.when(condition)
                def _():
                    detour.wait_recv()
                    onward.start()

            handed[0] += 2

        def blocks(ref, n):
            for l in range(2):
                for m in range(2):
                    yield l, m, ref.at[pl.ds(n * UNIT + l * BS, BS), pl.ds(m * BS, BS)]

        def mask_column(c):
            loads[c].wait()
            for ui in range(3):
                for l, m, block in blocks(own, c * 3 + ui):
                    keep = mask_x[0, 0, l, (ui * 3 + c) * 2 + m] > 0
                    value = staged[c, l, ui, m]
                    block[...] = jnp.where(keep, value, jnp.zeros_like(value))

        mask_column(0)
        to_left = send(own.at[unit(0, 3)], from_right, left)
        mask_column(2)
        to_right = send(own.at[unit(6, 3)], from_left, right)
        vertical = {}
        for c in (0, 2, 1):
            if c == 1:
                mask_column(c)
            vertical[c] = send_rows(own, c * 3, below, c * 3, 3, True, 0)
            vertical[c] += send_rows(own, c * 3, above, c * 3, 3, False, 0)

        row_of = {-1: above, 0: own, 1: below}
        filt_of = {
            -1: (filt_above, down_units), 0: (filtered, square_units), 1: (filt_below, up_units)
        }
        factor = {
            1: lambda p: from_left[unit(p + 1)],
            -1: lambda p: from_right[unit(p + 1)],
            0: lambda p: own[unit(given_at(p, 0))],
        }

        def product_square(q, t):
            total = None
            for p in (-1, 0, 1):
                u, v = t[0] - p, t[1] - q
                if abs(u) <= 1 and abs(v) <= 1:
                    term = jnp.dot(
                        factor[q](p), row_of[p][unit(given_at(u, v))],
                        preferred_element_type=jnp.float32,
                    )
                    total = term if total is None else total + term
            return total

        def product_cube(q, t):
            total = None
            for p in (-1, 0, 1):
                u, v = t[0] - p, t[1] - q
                if u * u + v * v <= 4:
                    ref, order = filt_of[p]
                    term = jnp.dot(
                        factor[q](p), ref[unit(order.index((u, v)))],
                        preferred_element_type=jnp.float32,
                    )
                    total = term if total is None else total + term
            return total

        def give(product, q, order, targets, buffer, landing, device):
            at = order.index(targets[0])
            for n, t in enumerate(targets):
                buffer[unit(at + n)] = product(q, t).astype(jnp.bfloat16)
            span = unit(at, len(targets))
            return send(buffer.at[span], landing.at[span], device)

        def give_left_square(targets):
            return give(product_square, 1, left_square, targets, give_left, got_right, left)

        def give_right_square(targets):
            return give(product_square, -1, right_square, targets, give_right, got_left, right)

        def finish_square(t, total):
            if t in left_square:
                part = got_right[unit(left_square.index(t))].astype(jnp.float32)
                total = part if total is None else total + part
            if t in right_square:
                part = got_left[unit(right_square.index(t))].astype(jnp.float32)
                total = part if total is None else total + part
            total = total * (0.25 / BS)
            for l, m, block in blocks(filtered, square_units.index(t)):
                keep = mask_sq[0, 0, l, square_slots.index(t) * 2 + m] > 0
                value = total[l * BS : (l + 1) * BS, m * BS : (m + 1) * BS]
                block[...] = jnp.where(keep, value, jnp.zeros_like(value)).astype(jnp.bfloat16)

        def send_filtered(units_up, units_down):
            copies = []
            for units, order, landing, goes_up in (
                (units_up, up_units, filt_below, True), (units_down, down_units, filt_above, False)
            ):
                copies += send_rows(
                    filtered, square_units.index(units[0]), landing, order.index(units[0]),
                    len(units), goes_up, 9,
                )
            return copies

        def await_recv(*groups):
            for group in groups:
                for copy in group:
                    copy.wait_recv()

        pass_on()
        pass_on()
        pass_on()
        await_recv(to_left, to_right)
        await_recv(vertical[0])
        r_far = give_right_square([(0, -2)])
        l_mid = give_left_square([(u, 0) for u in range(-2, 3)])
        await_recv(r_far)
        finish_square((0, -2), None)
        f_left = send_filtered([(0, -2)], [(0, -2)])
        await_recv(vertical[2])
        l_far = give_left_square([(0, 2)])
        r_mid = give_right_square([(u, 0) for u in range(-2, 3)])
        pass_on()
        await_recv(l_far)
        finish_square((0, 2), None)
        f_right = send_filtered([(0, 2)], [(0, 2)])
        for n, v in enumerate((-1, 1)):
            for u in (-1, 0, 1):
                acc[unit(n * 3 + u + 1)] = product_square(0, (u, v))
        pass_on()
        await_recv(vertical[1])
        near = []
        for u in (0, -1, 1):
            near += give_left_square([(u, 1)])
            near += give_right_square([(u, -1)])
        await_recv(l_mid, r_mid)
        for u in range(-2, 3):
            finish_square((u, 0), product_square(0, (u, 0)))
        f_mid = send_filtered([(u, 0) for u in (-2, -1, 0)], [(u, 0) for u in (0, 1, 2)])
        pass_on()
        await_recv(near)
        f_near = []
        for n, v in enumerate((-1, 1)):
            for u in (-1, 0, 1):
                finish_square((u, v), acc[unit(n * 3 + u + 1)])
            f_near.append(send_filtered([(u, v) for u in (-1, 0)], [(u, v) for u in (0, 1)]))
        pass_on()
        pass_on()

        def give_left_cube(v):
            return give(
                product_cube, 1, left_cube, [(u, v) for u in (-1, 0, 1)], give_left2, got_right2, left
            )

        def give_right_cube(v):
            return give(
                product_cube, -1, right_cube, [(u, v) for u in (-1, 0, 1)], give_right2, got_left2, right
            )

        def finish_cube(t, total):
            u, v = t
            total = total + got_right2[unit(left_cube.index(t))].astype(jnp.float32)
            total = total + got_left2[unit(right_cube.index(t))].astype(jnp.float32)
            total = 1.5 * own[unit(given_at(u, v))].astype(jnp.float32) - 0.5 * total
            for l in range(2):
                for m in range(2):
                    keep = mask_x[0, 0, l, ((u + 1) * 3 + v + 1) * 2 + m] > 0
                    value = total[l * BS : (l + 1) * BS, m * BS : (m + 1) * BS]
                    result[v + 1, l, u + 1, m] = jnp.where(keep, value, jnp.zeros_like(value)).astype(
                        jnp.bfloat16
                    )

        stores = []

        def store(v):
            copy = pltpu.make_async_copy(result.at[v + 1], out.at[:, :, v + 1], out_sem.at[v + 1])
            copy.start()
            stores.append(copy)

        await_recv(f_left)
        c_l = [give_left_cube(-1)]
        await_recv(f_right)
        c_r = [give_right_cube(1)]
        await_recv(f_mid)
        c_l.append(give_left_cube(1))
        c_r.append(give_right_cube(-1))
        for u in (-1, 0, 1):
            acc[unit(6 + u + 1)] = product_cube(0, (u, 0))
        await_recv(f_near[0])
        c_l.append(give_left_cube(0))
        await_recv(f_near[1])
        c_r.append(give_right_cube(0))
        await_recv(c_l[0], c_l[1], c_r[0], c_r[1])
        for v in (-1, 1):
            for u in (-1, 0, 1):
                finish_cube((u, v), product_cube(0, (u, v)))
            store(v)
        await_recv(c_l[2], c_r[2])
        for u in (-1, 0, 1):
            finish_cube((u, 0), acc[unit(6 + u + 1)])
        store(0)
        for copy in sent:
            copy.wait_send()
        for condition, _, onward in passed:

            @pl.when(condition)
            def _():
                onward.wait_send()

        for copy in stores:
            copy.wait()

    return kernel


def solution(mesh):
    rows, cols = mesh.shape["row"], mesh.shape["col"]

    def units(n, dtype=jnp.bfloat16):
        return pltpu.VMEM((n * UNIT, UNIT), dtype)

    def local(values, mask_x, mask_sq):
        grid = values.reshape(2, 3, 3, 2, BS, BS)
        out = pl.pallas_call(
            make_kernel(rows, cols),
            out_shape=jax.ShapeDtypeStruct(grid.shape, jnp.bfloat16),
            in_specs=[
                pl.BlockSpec(memory_space=pl.ANY),
                pl.BlockSpec(memory_space=pltpu.SMEM),
                pl.BlockSpec(memory_space=pltpu.SMEM),
            ],
            out_specs=pl.BlockSpec(memory_space=pl.ANY),
            scratch_shapes=[
                pltpu.VMEM((3, 2, 3, 2, BS, BS), jnp.bfloat16),
                units(9), units(9), units(9), units(3), units(3),
                units(9), units(9), units(9), units(9),
                units(13), units(9), units(9),
                units(9), units(9), units(9), units(9),
                units(18),
                units(9, jnp.float32),
                pltpu.VMEM((3, 2, 3, 2, BS, BS), jnp.bfloat16),
                pltpu.SemaphoreType.DMA((3,)),
                pltpu.SemaphoreType.DMA((3,)),
                pltpu.SemaphoreType.DMA((64,)),
                pltpu.SemaphoreType.DMA((64,)),
                pltpu.SemaphoreType.DMA((16,)),
                pltpu.SemaphoreType.DMA((16,)),
            ],
            compiler_params=pltpu.CompilerParams(
                collective_id=0, has_side_effects=True, vmem_limit_bytes=60 * 2**20
            ),
        )(grid, mask_x, mask_sq)
        return out.reshape(values.shape)

    return jax.shard_map(
        local,
        mesh=mesh,
        in_specs=(
            P("row", "col", None, None, None, None),
            P("row", "col", None, None),
            P("row", "col", None, None),
        ),
        out_specs=P("row", "col", None, None, None, None),
        check_vma=False,
    )
```

```python
import jax
import jax.numpy as jnp
from jax import lax
from jax.experimental import pallas as pl
from jax.experimental.pallas import tpu as pltpu
from jax.sharding import PartitionSpec as P

BS = 128
UNIT = 2 * BS
MESH = pl.DeviceIdType.MESH
X = 4

square_units = [(0, -2), (0, 2)] + [(u, 0) for u in range(-2, 3)]
square_units += [(u, -1) for u in (-1, 0, 1)] + [(u, 1) for u in (-1, 0, 1)]
up_units = [(0, -2), (0, 2)] + [(u, v) for v in (0, -1, 1) for u in (-1, 0)] + [(-2, 0)]
down_units = [(0, -2), (0, 2)] + [(u, v) for v in (0, -1, 1) for u in (0, 1)] + [(2, 0)]
square_slots = [(u, v) for u in range(-2, 3) for v in range(-2, 3) if u * u + v * v <= 4]

left_square = [(u, 0) for u in (-1, 0, 1)] + [(0, 2)] + [(u, 1) for u in (-1, 0, 1)]
right_square = [(u, 0) for u in (-1, 0, 1)] + [(0, -2)] + [(u, -1) for u in (-1, 0, 1)]
left_cube = [(u, v) for v in (-1, 1, 0) for u in (-1, 0, 1)]
right_cube = [(u, v) for v in (1, -1, 0) for u in (-1, 0, 1)]


def given_at(u, v):
    return (v + 1) * 3 + u + 1


def unit(n, count=1):
    return pl.ds(n * UNIT, count * UNIT)


def make_kernel(rows, cols):
    def kernel(
        values, mask_x, mask_sq, out,
        staged, own, above, below, from_left, from_right,
        give_left, give_right, got_left, got_right,
        filtered, filt_above, filt_below,
        give_left2, give_right2, got_left2, got_right2,
        passing, give_tip, tip_above, tip_below, acc, result, load_sem, out_sem, send_sem, recv_sem, pass_recv_sem, pass_send_sem,
    ):
        a, b = lax.axis_index("row"), lax.axis_index("col")

        def row(shift):
            return (lax.rem(a + shift + rows, rows), b)

        up, down = row(-1), row(1)
        left = (a, lax.rem(b + cols - 1, cols))
        right = (a, lax.rem(b + 1, cols))
        x = lax.rem(a, X)
        first, last = x == 0, x == X - 1

        loads = {}
        for c in (0, 2, 1):
            loads[c] = pltpu.make_async_copy(values.at[:, :, c], staged.at[c], load_sem.at[c])
            loads[c].start()

        barrier = pltpu.get_barrier_semaphore()

        def greet(device):
            pl.semaphore_signal(barrier, inc=1, device_id=device, device_id_type=MESH)

        for device in (up, down, left, right):
            greet(device)

        @pl.when(first)
        def _():
            greet(row(X - 1))
            greet(row(-X))

        @pl.when(last)
        def _():
            greet(row(1 - X))
            greet(row(X))

        pl.semaphore_wait(barrier, jnp.where(first | last, 6, 4))

        sent = []

        def make(src, dst, device):
            n = len(sent)
            copy = pltpu.make_async_remote_copy(
                src_ref=src, dst_ref=dst, send_sem=send_sem.at[n], recv_sem=recv_sem.at[n],
                device_id=device, device_id_type=MESH,
            )
            sent.append(copy)
            return copy

        def send(src, dst, device):
            copy = make(src, dst, device)
            copy.start()
            return [copy]

        passed = []

        def send_rows(src, src_unit, dst, dst_unit, count, goes_up, base):
            device, at_wrap, partner = (up, first, row(X - 1)) if goes_up else (down, last, row(1 - X))
            half = count * UNIT // 2
            straight = make(
                src.at[pl.ds(src_unit * UNIT, half)], dst.at[pl.ds(dst_unit * UNIT, half)], device
            )
            n = len(passed) // 2
            src_half = src.at[pl.ds(src_unit * UNIT + half, half)]
            dst_half = dst.at[pl.ds(dst_unit * UNIT + half, half)]
            hold = passing.at[pl.ds((base + dst_unit) * UNIT + half, half)]
            other = make(src_half, dst_half, device)
            k = len(sent) - 1
            detour = pltpu.make_async_remote_copy(
                src_ref=src_half, dst_ref=hold, send_sem=send_sem.at[k],
                recv_sem=pass_recv_sem.at[n], device_id=partner, device_id_type=MESH,
            )
            onward = pltpu.make_async_remote_copy(
                src_ref=hold, dst_ref=dst_half, send_sem=pass_send_sem.at[n],
                recv_sem=recv_sem.at[k], device_id=row(-X if goes_up else X), device_id_type=MESH,
            )
            passed.append((last if goes_up else first, detour, onward))
            straight.start()

            @pl.when(at_wrap)
            def _():
                detour.start()

            @pl.when(jnp.logical_not(at_wrap))
            def _():
                other.start()

            return [straight, other]

        handed = [0]

        def pass_on():
            for condition, detour, onward in passed[handed[0] : handed[0] + 2]:

                @pl.when(condition)
                def _():
                    detour.wait_recv()
                    onward.start()

            handed[0] += 2

        def blocks(ref, n):
            for l in range(2):
                for m in range(2):
                    yield l, m, ref.at[pl.ds(n * UNIT + l * BS, BS), pl.ds(m * BS, BS)]

        def mask_column(c):
            loads[c].wait()
            for ui in range(3):
                for l, m, block in blocks(own, c * 3 + ui):
                    keep = mask_x[0, 0, l, (ui * 3 + c) * 2 + m] > 0
                    value = staged[c, l, ui, m]
                    block[...] = jnp.where(keep, value, jnp.zeros_like(value))

        mask_column(0)
        to_left = send(own.at[unit(0, 3)], from_right, left)
        mask_column(2)
        to_right = send(own.at[unit(6, 3)], from_left, right)
        vertical = {}
        for c in (0, 2, 1):
            if c == 1:
                mask_column(c)
            vertical[c] = send_rows(own, c * 3, below, c * 3, 2, True, 0)
            vertical[c] += send_rows(own, c * 3 + 1, above, c * 3 + 1, 2, False, 0)

        row_of = {-1: above, 0: own, 1: below}
        filt_of = {
            -1: (filt_above, down_units), 0: (filtered, square_units), 1: (filt_below, up_units)
        }
        factor = {
            1: lambda p: from_left[unit(p + 1)],
            -1: lambda p: from_right[unit(p + 1)],
            0: lambda p: own[unit(given_at(p, 0))],
        }

        def product_square(q, t):
            total = None
            for p in (-1, 0, 1):
                u, v = t[0] - p, t[1] - q
                if abs(u) <= 1 and abs(v) <= 1:
                    term = jnp.dot(
                        factor[q](p), row_of[p][unit(given_at(u, v))],
                        preferred_element_type=jnp.float32,
                    )
                    total = term if total is None else total + term
            return total

        def product_tip(p):
            total = None
            for q in (-1, 0, 1):
                right_factor = (from_left, own, from_right)[q + 1]
                at = given_at(p, 0) if q == 0 else p + 1
                term = jnp.dot(
                    (below, above)[(p + 1) // 2][unit(given_at(p, q))], right_factor[unit(at)],
                    preferred_element_type=jnp.float32,
                )
                total = term if total is None else total + term
            return total

        def product_cube(q, t):
            total = None
            for p in (-1, 0, 1):
                u, v = t[0] - p, t[1] - q
                if u * u + v * v <= 4:
                    ref, order = filt_of[p]
                    term = jnp.dot(
                        factor[q](p), ref[unit(order.index((u, v)))],
                        preferred_element_type=jnp.float32,
                    )
                    total = term if total is None else total + term
            return total

        def give(product, q, order, targets, buffer, landing, device):
            at = order.index(targets[0])
            for n, t in enumerate(targets):
                buffer[unit(at + n)] = product(q, t).astype(jnp.bfloat16)
            span = unit(at, len(targets))
            return send(buffer.at[span], landing.at[span], device)

        def give_left_square(targets):
            return give(product_square, 1, left_square, targets, give_left, got_right, left)

        def give_right_square(targets):
            return give(product_square, -1, right_square, targets, give_right, got_left, right)

        def finish_square(t, total):
            if t in left_square:
                part = got_right[unit(left_square.index(t))].astype(jnp.float32)
                total = part if total is None else total + part
            if t in right_square:
                part = got_left[unit(right_square.index(t))].astype(jnp.float32)
                total = part if total is None else total + part
            total = total * (0.25 / BS)
            for l, m, block in blocks(filtered, square_units.index(t)):
                keep = mask_sq[0, 0, l, square_slots.index(t) * 2 + m] > 0
                value = total[l * BS : (l + 1) * BS, m * BS : (m + 1) * BS]
                block[...] = jnp.where(keep, value, jnp.zeros_like(value)).astype(jnp.bfloat16)

        def send_filtered(units_up, units_down):
            copies = []
            for units, order, landing, goes_up in (
                (units_up, up_units, filt_below, True), (units_down, down_units, filt_above, False)
            ):
                copies += send_rows(
                    filtered, square_units.index(units[0]), landing, order.index(units[0]),
                    len(units), goes_up, 9,
                )
            return copies

        def await_recv(*groups):
            for group in groups:
                for copy in group:
                    copy.wait_recv()

        pass_on()
        pass_on()
        pass_on()
        await_recv(to_left, to_right)
        await_recv(vertical[0])
        r_far = give_right_square([(0, -2)])
        l_mid = give_left_square([(u, 0) for u in (-1, 0, 1)])
        await_recv(r_far)
        finish_square((0, -2), None)
        f_left = send_filtered([(0, -2)], [(0, -2)])
        await_recv(vertical[2])
        l_far = give_left_square([(0, 2)])
        r_mid = give_right_square([(u, 0) for u in (-1, 0, 1)])
        pass_on()
        await_recv(l_far)
        finish_square((0, 2), None)
        f_right = send_filtered([(0, 2)], [(0, 2)])
        for n, v in enumerate((-1, 1)):
            for u in (-1, 0, 1):
                acc[unit(n * 3 + u + 1)] = product_square(0, (u, v))
        pass_on()
        await_recv(vertical[1])
        for n, p in enumerate((1, -1)):
            give_tip[unit(n)] = product_tip(p).astype(jnp.bfloat16)
        tips = send_rows(give_tip, 0, tip_below, 0, 1, True, 18)
        tips += send_rows(give_tip, 1, tip_above, 0, 1, False, 18)
        near = []
        for u in (0, -1, 1):
            near += give_left_square([(u, 1)])
            near += give_right_square([(u, -1)])
        pass_on()
        await_recv(l_mid, r_mid)
        for u in (-1, 0, 1):
            finish_square((u, 0), product_square(0, (u, 0)))
        f_mid = send_filtered([(u, 0) for u in (-1, 0)], [(u, 0) for u in (0, 1)])
        pass_on()
        await_recv(near)
        f_near = []
        for n, v in enumerate((-1, 1)):
            for u in (-1, 0, 1):
                finish_square((u, v), acc[unit(n * 3 + u + 1)])
            f_near.append(send_filtered([(u, v) for u in (-1, 0)], [(u, v) for u in (0, 1)]))
        pass_on()
        pass_on()

        await_recv(tips)
        for u, tip in ((-2, tip_above), (2, tip_below)):
            finish_square((u, 0), tip[...].astype(jnp.float32))
        f_tip = send_filtered([(-2, 0)], [(2, 0)])
        pass_on()

        def give_left_cube(v):
            return give(
                product_cube, 1, left_cube, [(u, v) for u in (-1, 0, 1)], give_left2, got_right2, left
            )

        def give_right_cube(v):
            return give(
                product_cube, -1, right_cube, [(u, v) for u in (-1, 0, 1)], give_right2, got_left2, right
            )

        def finish_cube(t, total):
            u, v = t
            total = total + got_right2[unit(left_cube.index(t))].astype(jnp.float32)
            total = total + got_left2[unit(right_cube.index(t))].astype(jnp.float32)
            total = 1.5 * own[unit(given_at(u, v))].astype(jnp.float32) - 0.5 * total
            for l in range(2):
                for m in range(2):
                    keep = mask_x[0, 0, l, ((u + 1) * 3 + v + 1) * 2 + m] > 0
                    value = total[l * BS : (l + 1) * BS, m * BS : (m + 1) * BS]
                    result[v + 1, l, u + 1, m] = jnp.where(keep, value, jnp.zeros_like(value)).astype(
                        jnp.bfloat16
                    )

        stores = []

        def store(v):
            copy = pltpu.make_async_copy(result.at[v + 1], out.at[:, :, v + 1], out_sem.at[v + 1])
            copy.start()
            stores.append(copy)

        await_recv(f_left)
        c_far = [give_left_cube(-1)]
        await_recv(f_right)
        c_far += [give_right_cube(1)]
        await_recv(f_mid, f_near[0])
        c_near = [give_left_cube(0)]
        await_recv(f_near[1])
        c_near += [give_right_cube(0)]
        await_recv(f_tip)
        c_mid = [give_left_cube(1), give_right_cube(-1)]
        for u in (-1, 0, 1):
            acc[unit(6 + u + 1)] = product_cube(0, (u, 0))
        await_recv(*c_far)
        await_recv(*c_near)
        for u in (-1, 0, 1):
            finish_cube((u, 0), acc[unit(6 + u + 1)])
        store(0)
        for v in (-1, 1):
            for u in (-1, 0, 1):
                acc[unit((v + 1) // 2 * 3 + u + 1)] = product_cube(0, (u, v))
        await_recv(*c_mid)
        for v in (-1, 1):
            for u in (-1, 0, 1):
                finish_cube((u, v), acc[unit((v + 1) // 2 * 3 + u + 1)])
            store(v)
        for copy in sent:
            copy.wait_send()
        for condition, _, onward in passed:

            @pl.when(condition)
            def _():
                onward.wait_send()

        for copy in stores:
            copy.wait()

    return kernel


def solution(mesh):
    rows, cols = mesh.shape["row"], mesh.shape["col"]

    def units(n, dtype=jnp.bfloat16):
        return pltpu.VMEM((n * UNIT, UNIT), dtype)

    def local(values, mask_x, mask_sq):
        grid = values.reshape(2, 3, 3, 2, BS, BS)
        out = pl.pallas_call(
            make_kernel(rows, cols),
            out_shape=jax.ShapeDtypeStruct(grid.shape, jnp.bfloat16),
            in_specs=[
                pl.BlockSpec(memory_space=pl.ANY),
                pl.BlockSpec(memory_space=pltpu.SMEM),
                pl.BlockSpec(memory_space=pltpu.SMEM),
            ],
            out_specs=pl.BlockSpec(memory_space=pl.ANY),
            scratch_shapes=[
                pltpu.VMEM((3, 2, 3, 2, BS, BS), jnp.bfloat16),
                units(9), units(9), units(9), units(3), units(3),
                units(7), units(7), units(7), units(7),
                units(13), units(9), units(9),
                units(9), units(9), units(9), units(9),
                units(19), units(2), units(1), units(1),
                units(9, jnp.float32),
                pltpu.VMEM((3, 2, 3, 2, BS, BS), jnp.bfloat16),
                pltpu.SemaphoreType.DMA((3,)),
                pltpu.SemaphoreType.DMA((3,)),
                pltpu.SemaphoreType.DMA((64,)),
                pltpu.SemaphoreType.DMA((64,)),
                pltpu.SemaphoreType.DMA((16,)),
                pltpu.SemaphoreType.DMA((16,)),
            ],
            compiler_params=pltpu.CompilerParams(
                collective_id=0, has_side_effects=True, vmem_limit_bytes=60 * 2**20
            ),
        )(grid, mask_x, mask_sq)
        return out.reshape(values.shape)

    return jax.shard_map(
        local,
        mesh=mesh,
        in_specs=(
            P("row", "col", None, None, None, None),
            P("row", "col", None, None),
            P("row", "col", None, None),
        ),
        out_specs=P("row", "col", None, None, None, None),
        check_vma=False,
    )
```

```python
import jax
import jax.numpy as jnp
from jax import lax
from jax.experimental import pallas as pl
from jax.experimental.pallas import tpu as pltpu
from jax.sharding import PartitionSpec as P

BS = 128
UNIT = 2 * BS
MESH = pl.DeviceIdType.MESH
X = 4

square_units = [(-1, 0), (0, -2), (0, 2), (0, 0), (1, 0)]
square_units += [(u, v) for u in (-1, 0, 1) for v in (-1, 1)] + [(-2, 0), (2, 0)]
up_units = square_units[0:4] + square_units[5:9] + [(-2, 0)]
down_units = square_units[1:5] + square_units[7:11] + [(2, 0)]

square_slots = [(u, v) for u in range(-2, 3) for v in range(-2, 3) if u * u + v * v <= 4]

left_square = [(u, 0) for u in (-1, 0, 1)] + [(0, 2)] + [(u, 1) for u in (-1, 0, 1)]
right_square = [(u, 0) for u in (-1, 0, 1)] + [(0, -2)] + [(u, -1) for u in (-1, 0, 1)]
left_cube = [(u, v) for v in (-1, 1, 0) for u in (-1, 0, 1)]
right_cube = [(u, v) for v in (1, -1, 0) for u in (-1, 0, 1)]


def given_at(u, v):
    return (v + 1) * 3 + u + 1


def unit(n, count=1):
    return pl.ds(n * UNIT, count * UNIT)


def make_kernel(rows, cols):
    def kernel(
        values, mask_x_in, mask_sq_in, out,
        mask_x, mask_sq, staged, own, above, below, from_left, from_right,
        give_left, give_right, got_left, got_right,
        filtered, filt_above, filt_below,
        give_left2, give_right2, got_left2, got_right2,
        passing, give_tip, tip_above, tip_below, acc, load_sem, send_sem, recv_sem, pass_recv_sem, pass_send_sem,
    ):
        a, b = lax.axis_index("row"), lax.axis_index("col")

        def row(shift):
            return (lax.rem(a + shift + rows, rows), b)

        up, down = row(-1), row(1)
        left = (a, lax.rem(b + cols - 1, cols))
        right = (a, lax.rem(b + 1, cols))
        x = lax.rem(a, X)
        first, last = x == 0, x == X - 1

        loads = {}
        for c in (0, 2, 1):
            loads[c] = pltpu.make_async_copy(values.at[:, :, c], staged.at[c], load_sem.at[c])
            loads[c].start()
        masks = [
            pltpu.make_async_copy(mask_x_in, mask_x, load_sem.at[3]),
            pltpu.make_async_copy(mask_sq_in, mask_sq, load_sem.at[4]),
        ]
        for copy in masks:
            copy.start()

        barrier = pltpu.get_barrier_semaphore()

        def greet(device):
            pl.semaphore_signal(barrier, inc=1, device_id=device, device_id_type=MESH)

        for device in (up, down, left, right):
            greet(device)

        @pl.when(first)
        def _():
            greet(row(X - 1))
            greet(row(-X))

        @pl.when(last)
        def _():
            greet(row(1 - X))
            greet(row(X))

        pl.semaphore_wait(barrier, jnp.where(first | last, 6, 4))

        sent = []

        def make(src, dst, device):
            n = len(sent)
            copy = pltpu.make_async_remote_copy(
                src_ref=src, dst_ref=dst, send_sem=send_sem.at[n], recv_sem=recv_sem.at[n],
                device_id=device, device_id_type=MESH,
            )
            sent.append(copy)
            return copy

        def send(src, dst, device):
            copy = make(src, dst, device)
            copy.start()
            return [copy]

        passed = []

        def send_rows(src, src_unit, dst, dst_unit, count, goes_up, base):
            device, at_wrap, partner = (up, first, row(X - 1)) if goes_up else (down, last, row(1 - X))
            half = count * UNIT // 2
            straight = make(
                src.at[pl.ds(src_unit * UNIT, half)], dst.at[pl.ds(dst_unit * UNIT, half)], device
            )
            n = len(passed) // 2
            src_half = src.at[pl.ds(src_unit * UNIT + half, half)]
            dst_half = dst.at[pl.ds(dst_unit * UNIT + half, half)]
            hold = passing.at[pl.ds((base + dst_unit) * UNIT + half, half)]
            other = make(src_half, dst_half, device)
            k = len(sent) - 1
            detour = pltpu.make_async_remote_copy(
                src_ref=src_half, dst_ref=hold, send_sem=send_sem.at[k],
                recv_sem=pass_recv_sem.at[n], device_id=partner, device_id_type=MESH,
            )
            onward = pltpu.make_async_remote_copy(
                src_ref=hold, dst_ref=dst_half, send_sem=pass_send_sem.at[n],
                recv_sem=recv_sem.at[k], device_id=row(-X if goes_up else X), device_id_type=MESH,
            )
            passed.append((last if goes_up else first, detour, onward))
            straight.start()

            @pl.when(at_wrap)
            def _():
                detour.start()

            @pl.when(jnp.logical_not(at_wrap))
            def _():
                other.start()

            return [straight, other]

        handed = [0]

        def pass_on():
            for condition, detour, onward in passed[handed[0] : handed[0] + 2]:

                @pl.when(condition)
                def _():
                    detour.wait_recv()
                    onward.start()

            handed[0] += 2

        def blocks(ref, n):
            for l in range(2):
                for m in range(2):
                    yield l, m, ref.at[pl.ds(n * UNIT + l * BS, BS), pl.ds(m * BS, BS)]

        for copy in masks:
            copy.wait()

        def mask_column(c):
            loads[c].wait()
            for ui in range(3):
                for l, m, block in blocks(own, c * 3 + ui):
                    keep = mask_x[0, 0, l, (ui * 3 + c) * 2 + m] > 0
                    value = staged[c, l, ui, m]
                    block[...] = jnp.where(keep, value, jnp.zeros_like(value))

        mask_column(0)
        to_left = send(own.at[unit(0, 3)], from_right, left)
        mask_column(2)
        to_right = send(own.at[unit(6, 3)], from_left, right)
        vertical = {}
        for c in (0, 2, 1):
            if c == 1:
                mask_column(c)
            vertical[c] = send_rows(own, c * 3, below, c * 3, 2, True, 0)
            vertical[c] += send_rows(own, c * 3 + 1, above, c * 3 + 1, 2, False, 0)

        row_of = {-1: above, 0: own, 1: below}
        filt_of = {
            -1: (filt_above, down_units), 0: (filtered, square_units), 1: (filt_below, up_units)
        }
        factor = {
            1: lambda p: from_left[unit(p + 1)],
            -1: lambda p: from_right[unit(p + 1)],
            0: lambda p: own[unit(given_at(p, 0))],
        }

        def product_square(q, t):
            total = None
            for p in (-1, 0, 1):
                u, v = t[0] - p, t[1] - q
                if abs(u) <= 1 and abs(v) <= 1:
                    term = jnp.dot(
                        factor[q](p), row_of[p][unit(given_at(u, v))],
                        preferred_element_type=jnp.float32,
                    )
                    total = term if total is None else total + term
            return total

        def product_tip(p):
            total = None
            for q in (-1, 0, 1):
                right_factor = (from_left, own, from_right)[q + 1]
                at = given_at(p, 0) if q == 0 else p + 1
                term = jnp.dot(
                    (below, above)[(p + 1) // 2][unit(given_at(p, q))], right_factor[unit(at)],
                    preferred_element_type=jnp.float32,
                )
                total = term if total is None else total + term
            return total

        def product_cube(q, t):
            total = None
            for p in (-1, 0, 1):
                u, v = t[0] - p, t[1] - q
                if u * u + v * v <= 4:
                    ref, order = filt_of[p]
                    term = jnp.dot(
                        factor[q](p), ref[unit(order.index((u, v)))],
                        preferred_element_type=jnp.float32,
                    )
                    total = term if total is None else total + term
            return total

        def give(product, q, order, targets, buffer, landing, device):
            at = order.index(targets[0])
            for n, t in enumerate(targets):
                buffer[unit(at + n)] = product(q, t).astype(jnp.bfloat16)
            span = unit(at, len(targets))
            return send(buffer.at[span], landing.at[span], device)

        def give_left_square(targets):
            return give(product_square, 1, left_square, targets, give_left, got_right, left)

        def give_right_square(targets):
            return give(product_square, -1, right_square, targets, give_right, got_left, right)

        def finish_square(t, total):
            if t in left_square:
                part = got_right[unit(left_square.index(t))].astype(jnp.float32)
                total = part if total is None else total + part
            if t in right_square:
                part = got_left[unit(right_square.index(t))].astype(jnp.float32)
                total = part if total is None else total + part
            total = total * (0.25 / BS)
            for l, m, block in blocks(filtered, square_units.index(t)):
                keep = mask_sq[0, 0, l, square_slots.index(t) * 2 + m] > 0
                value = total[l * BS : (l + 1) * BS, m * BS : (m + 1) * BS]
                block[...] = jnp.where(keep, value, jnp.zeros_like(value)).astype(jnp.bfloat16)

        def send_filtered(units_up, units_down):
            copies = []
            for units, order, landing, goes_up in (
                (units_up, up_units, filt_below, True), (units_down, down_units, filt_above, False)
            ):
                copies += send_rows(
                    filtered, square_units.index(units[0]), landing, order.index(units[0]),
                    len(units), goes_up, 9,
                )
            return copies

        def await_recv(*groups):
            for group in groups:
                for copy in group:
                    copy.wait_recv()

        pass_on()
        pass_on()
        pass_on()
        await_recv(to_left, to_right)
        await_recv(vertical[0])
        far = give_right_square([(0, -2)])
        mid = give_left_square([(u, 0) for u in (-1, 0, 1)])
        await_recv(vertical[2])
        far += give_left_square([(0, 2)])
        mid += give_right_square([(u, 0) for u in (-1, 0, 1)])
        await_recv(vertical[1])
        for n, p in enumerate((1, -1)):
            give_tip[unit(n)] = product_tip(p).astype(jnp.bfloat16)
        tips = send_rows(give_tip, 0, tip_below, 0, 1, True, 18)
        tips += send_rows(give_tip, 1, tip_above, 0, 1, False, 18)
        near = []
        for u in (0, -1, 1):
            near += give_left_square([(u, 1)])
            near += give_right_square([(u, -1)])
        pass_on()
        for n, v in enumerate((-1, 1)):
            for u in (-1, 0, 1):
                acc[unit(n * 3 + u + 1)] = product_square(0, (u, v))
        await_recv(far, mid)
        finish_square((0, -2), None)
        finish_square((0, 2), None)
        for u in (-1, 0, 1):
            finish_square((u, 0), product_square(0, (u, 0)))
        f_mid = send_filtered(up_units[0:4], down_units[0:4])
        pass_on()
        await_recv(near)
        for n, v in enumerate((-1, 1)):
            for u in (-1, 0, 1):
                finish_square((u, v), acc[unit(n * 3 + u + 1)])
        f_near = send_filtered(up_units[4:8], down_units[4:8])
        await_recv(tips)
        for u, tip in ((-2, tip_above), (2, tip_below)):
            finish_square((u, 0), tip[...].astype(jnp.float32))
        f_tip = send_filtered([(-2, 0)], [(2, 0)])
        pass_on()
        pass_on()

        def give_left_cube(v):
            return give(
                product_cube, 1, left_cube, [(u, v) for u in (-1, 0, 1)], give_left2, got_right2, left
            )

        def give_right_cube(v):
            return give(
                product_cube, -1, right_cube, [(u, v) for u in (-1, 0, 1)], give_right2, got_left2, right
            )

        def finish_cube(t, total):
            u, v = t
            total = total + got_right2[unit(left_cube.index(t))].astype(jnp.float32)
            total = total + got_left2[unit(right_cube.index(t))].astype(jnp.float32)
            total = 1.5 * own[unit(given_at(u, v))].astype(jnp.float32) - 0.5 * total
            for l in range(2):
                for m in range(2):
                    keep = mask_x[0, 0, l, ((u + 1) * 3 + v + 1) * 2 + m] > 0
                    value = total[l * BS : (l + 1) * BS, m * BS : (m + 1) * BS]
                    out[l, u + 1, v + 1, m] = jnp.where(keep, value, jnp.zeros_like(value)).astype(
                        jnp.bfloat16
                    )

        await_recv(f_mid)
        c_far = [give_left_cube(-1), give_right_cube(1)]
        await_recv(f_near)
        c_near = [give_left_cube(0)]
        c_near += [give_right_cube(0)]
        await_recv(f_tip)
        c_mid = [give_left_cube(1), give_right_cube(-1)]
        for u in (-1, 0, 1):
            acc[unit(6 + u + 1)] = product_cube(0, (u, 0))
        await_recv(*c_far)
        await_recv(*c_near)
        for u in (-1, 0, 1):
            finish_cube((u, 0), acc[unit(6 + u + 1)])
        for v in (-1, 1):
            for u in (-1, 0, 1):
                acc[unit((v + 1) // 2 * 3 + u + 1)] = product_cube(0, (u, v))
        await_recv(*c_mid)
        for v in (-1, 1):
            for u in (-1, 0, 1):
                finish_cube((u, v), acc[unit((v + 1) // 2 * 3 + u + 1)])
        for copy in sent:
            copy.wait_send()
        for condition, _, onward in passed:

            @pl.when(condition)
            def _():
                onward.wait_send()


    return kernel


def solution(mesh):
    rows, cols = mesh.shape["row"], mesh.shape["col"]

    def units(n, dtype=jnp.bfloat16):
        return pltpu.VMEM((n * UNIT, UNIT), dtype)

    def local(values, mask_x, mask_sq):
        grid = values.reshape(2, 3, 3, 2, BS, BS)
        out = pl.pallas_call(
            make_kernel(rows, cols),
            out_shape=jax.ShapeDtypeStruct(grid.shape, jnp.bfloat16),
            in_specs=[
                pl.BlockSpec(memory_space=pltpu.HBM),
                pl.BlockSpec(memory_space=pltpu.HBM),
                pl.BlockSpec(memory_space=pltpu.HBM),
            ],
            out_specs=pl.BlockSpec(memory_space=pltpu.VMEM),
            scratch_shapes=[
                pltpu.SMEM(mask_x.shape, mask_x.dtype), pltpu.SMEM(mask_sq.shape, mask_sq.dtype),
                pltpu.VMEM((3, 2, 3, 2, BS, BS), jnp.bfloat16),
                units(9), units(9), units(9), units(3), units(3),
                units(7), units(7), units(7), units(7),
                units(13), units(9), units(9),
                units(9), units(9), units(9), units(9),
                units(19), units(2), units(1), units(1),
                units(9, jnp.float32),
                pltpu.SemaphoreType.DMA((5,)),
                pltpu.SemaphoreType.DMA((64,)),
                pltpu.SemaphoreType.DMA((64,)),
                pltpu.SemaphoreType.DMA((16,)),
                pltpu.SemaphoreType.DMA((16,)),
            ],
            compiler_params=pltpu.CompilerParams(
                collective_id=0, has_side_effects=True, vmem_limit_bytes=52 * 2**20
            ),
        )(grid, mask_x, mask_sq)
        return out.reshape(values.shape)

    return jax.shard_map(
        local,
        mesh=mesh,
        in_specs=(
            P("row", "col", None, None, None, None),
            P("row", "col", None, None),
            P("row", "col", None, None),
        ),
        out_specs=P("row", "col", None, None, None, None),
        check_vma=False,
    )
```

```python
import jax
import jax.numpy as jnp
from jax import lax
from jax.experimental import pallas as pl
from jax.experimental.pallas import tpu as pltpu
from jax.sharding import PartitionSpec as P

BS = 128
UNIT = 2 * BS
MESH = pl.DeviceIdType.MESH
X = 4

up_units = [(-1, 0), (-1, -1), (-1, 1), (-2, 0)]
down_units = [(1, 0), (1, -1), (1, 1), (2, 0)]
square_units = [(0, -2), (0, 0), (0, 2), (0, -1), (0, 1)] + up_units + down_units
side_left_units = [(0, 0), (0, 2), (0, 1)]
side_right_units = [(0, -2), (0, 0), (0, -1)]
square_slots = [(u, v) for u in range(-2, 3) for v in range(-2, 3) if u * u + v * v <= 4]

left_square = [(u, 0) for u in (-1, 0, 1)] + [(0, 2)] + [(u, 1) for u in (-1, 0, 1)]
right_square = [(u, 0) for u in (-1, 0, 1)] + [(0, -2)] + [(u, -1) for u in (-1, 0, 1)]
left_cube = [(0, -1)] + [(u, v) for v in (0, 1) for u in (-1, 0, 1)]
right_cube = [(0, 1)] + [(u, v) for v in (0, -1) for u in (-1, 0, 1)]


def given_at(u, v):
    return (v + 1) * 3 + u + 1


def unit(n, count=1):
    return pl.ds(n * UNIT, count * UNIT)


def make_kernel(rows, cols):
    def kernel(
        values, mask_x_in, mask_sq_in, out,
        mask_x, mask_sq, staged, own, above, below, from_left, from_right,
        give_left, give_right, got_left, got_right,
        filtered, filt_above, filt_below,
        give_left2, give_right2, got_left2, got_right2,
        passing, give_tip, tip_above, tip_below, side_left, side_right, give_rim, rim_above, rim_below, acc, load_sem, send_sem, recv_sem, pass_recv_sem, pass_send_sem,
    ):
        a, b = lax.axis_index("row"), lax.axis_index("col")

        def row(shift):
            return (lax.rem(a + shift + rows, rows), b)

        up, down = row(-1), row(1)
        left = (a, lax.rem(b + cols - 1, cols))
        right = (a, lax.rem(b + 1, cols))
        x = lax.rem(a, X)
        first, last = x == 0, x == X - 1

        loads = {}
        for c in (0, 2, 1):
            loads[c] = pltpu.make_async_copy(values.at[:, :, c], staged.at[c], load_sem.at[c])
            loads[c].start()
        masks = [
            pltpu.make_async_copy(mask_x_in, mask_x, load_sem.at[3]),
            pltpu.make_async_copy(mask_sq_in, mask_sq, load_sem.at[4]),
        ]
        for copy in masks:
            copy.start()

        barrier = pltpu.get_barrier_semaphore()

        def greet(device):
            pl.semaphore_signal(barrier, inc=1, device_id=device, device_id_type=MESH)

        for device in (up, down, left, right):
            greet(device)

        @pl.when(first)
        def _():
            greet(row(X - 1))
            greet(row(-X))

        @pl.when(last)
        def _():
            greet(row(1 - X))
            greet(row(X))

        pl.semaphore_wait(barrier, jnp.where(first | last, 6, 4))

        sent = []

        def make(src, dst, device):
            n = len(sent)
            copy = pltpu.make_async_remote_copy(
                src_ref=src, dst_ref=dst, send_sem=send_sem.at[n], recv_sem=recv_sem.at[n],
                device_id=device, device_id_type=MESH,
            )
            sent.append(copy)
            return copy

        def send(src, dst, device):
            copy = make(src, dst, device)
            copy.start()
            return [copy]

        passed = []

        def send_rows(src, src_unit, dst, dst_unit, count, goes_up, base):
            device, at_wrap, partner = (up, first, row(X - 1)) if goes_up else (down, last, row(1 - X))
            half = count * UNIT // 2
            straight = make(
                src.at[pl.ds(src_unit * UNIT, half)], dst.at[pl.ds(dst_unit * UNIT, half)], device
            )
            n = len(passed) // 2
            src_half = src.at[pl.ds(src_unit * UNIT + half, half)]
            dst_half = dst.at[pl.ds(dst_unit * UNIT + half, half)]
            hold = passing.at[pl.ds((base + dst_unit) * UNIT + half, half)]
            other = make(src_half, dst_half, device)
            k = len(sent) - 1
            detour = pltpu.make_async_remote_copy(
                src_ref=src_half, dst_ref=hold, send_sem=send_sem.at[k],
                recv_sem=pass_recv_sem.at[n], device_id=partner, device_id_type=MESH,
            )
            onward = pltpu.make_async_remote_copy(
                src_ref=hold, dst_ref=dst_half, send_sem=pass_send_sem.at[n],
                recv_sem=recv_sem.at[k], device_id=row(-X if goes_up else X), device_id_type=MESH,
            )
            passed.append((last if goes_up else first, detour, onward))
            straight.start()

            @pl.when(at_wrap)
            def _():
                detour.start()

            @pl.when(jnp.logical_not(at_wrap))
            def _():
                other.start()

            return [straight, other]

        handed = [0]

        def pass_on():
            for condition, detour, onward in passed[handed[0] : handed[0] + 2]:

                @pl.when(condition)
                def _():
                    detour.wait_recv()
                    onward.start()

            handed[0] += 2

        def blocks(ref, n):
            for l in range(2):
                for m in range(2):
                    yield l, m, ref.at[pl.ds(n * UNIT + l * BS, BS), pl.ds(m * BS, BS)]

        for copy in masks:
            copy.wait()

        def mask_column(c):
            loads[c].wait()
            for ui in range(3):
                for l, m, block in blocks(own, c * 3 + ui):
                    keep = mask_x[0, 0, l, (ui * 3 + c) * 2 + m] > 0
                    value = staged[c, l, ui, m]
                    block[...] = jnp.where(keep, value, jnp.zeros_like(value))

        mask_column(0)
        to_left = send(own.at[unit(0, 3)], from_right, left)
        mask_column(2)
        to_right = send(own.at[unit(6, 3)], from_left, right)
        vertical = {}
        for c in (0, 2, 1):
            if c == 1:
                mask_column(c)
            vertical[c] = send_rows(own, c * 3, below, c * 3, 2, True, 0)
            vertical[c] += send_rows(own, c * 3 + 1, above, c * 3 + 1, 2, False, 0)

        row_of = {-1: above, 0: own, 1: below}
        filt_of = {
            -1: (filt_above, down_units), 0: (filtered, square_units), 1: (filt_below, up_units)
        }
        factor = {
            1: lambda p: from_left[unit(p + 1)],
            -1: lambda p: from_right[unit(p + 1)],
            0: lambda p: own[unit(given_at(p, 0))],
        }

        def product_square(q, t):
            total = None
            for p in (-1, 0, 1):
                u, v = t[0] - p, t[1] - q
                if abs(u) <= 1 and abs(v) <= 1:
                    term = jnp.dot(
                        factor[q](p), row_of[p][unit(given_at(u, v))],
                        preferred_element_type=jnp.float32,
                    )
                    total = term if total is None else total + term
            return total

        def product_tip(p):
            total = None
            for q in (-1, 0, 1):
                right_factor = (from_left, own, from_right)[q + 1]
                at = given_at(p, 0) if q == 0 else p + 1
                term = jnp.dot(
                    (below, above)[(p + 1) // 2][unit(given_at(p, q))], right_factor[unit(at)],
                    preferred_element_type=jnp.float32,
                )
                total = term if total is None else total + term
            return total

        def product_cube(q, t):
            total = None
            for p in (-1, 0, 1):
                u, v = t[0] - p, t[1] - q
                if u * u + v * v <= 4 and (p == 0 or u != 0):
                    ref, order = filt_of[p]
                    term = jnp.dot(
                        factor[q](p), ref[unit(order.index((u, v)))],
                        preferred_element_type=jnp.float32,
                    )
                    total = term if total is None else total + term
            return total

        def product_rim(p, v):
            total = None
            for q in (-1, 0, 1):
                ref, order = (
                    (side_left, side_left_units), (filtered, square_units), (side_right, side_right_units)
                )[q + 1]
                term = jnp.dot(
                    (below, above)[(p + 1) // 2][unit(given_at(p, q))], ref[unit(order.index((0, v - q)))],
                    preferred_element_type=jnp.float32,
                )
                total = term if total is None else total + term
            return total

        def give(product, q, order, targets, buffer, landing, device):
            at = order.index(targets[0])
            for n, t in enumerate(targets):
                buffer[unit(at + n)] = product(q, t).astype(jnp.bfloat16)
            span = unit(at, len(targets))
            return send(buffer.at[span], landing.at[span], device)

        def give_left_square(targets):
            return give(product_square, 1, left_square, targets, give_left, got_right, left)

        def give_right_square(targets):
            return give(product_square, -1, right_square, targets, give_right, got_left, right)

        def finish_square(t, total):
            if t in left_square:
                part = got_right[unit(left_square.index(t))].astype(jnp.float32)
                total = part if total is None else total + part
            if t in right_square:
                part = got_left[unit(right_square.index(t))].astype(jnp.float32)
                total = part if total is None else total + part
            total = total * (0.25 / BS)
            for l, m, block in blocks(filtered, square_units.index(t)):
                keep = mask_sq[0, 0, l, square_slots.index(t) * 2 + m] > 0
                value = total[l * BS : (l + 1) * BS, m * BS : (m + 1) * BS]
                block[...] = jnp.where(keep, value, jnp.zeros_like(value)).astype(jnp.bfloat16)

        def send_filtered(units_up, units_down):
            copies = []
            for units, order, landing, goes_up in (
                (units_up, up_units, filt_below, True), (units_down, down_units, filt_above, False)
            ):
                copies += send_rows(
                    filtered, square_units.index(units[0]), landing, order.index(units[0]),
                    len(units), goes_up, 9,
                )
            return copies

        def await_recv(*groups):
            for group in groups:
                for copy in group:
                    copy.wait_recv()

        pass_on()
        pass_on()
        pass_on()
        await_recv(to_left, to_right)
        await_recv(vertical[0])
        far = give_right_square([(0, -2)])
        mid = give_left_square([(u, 0) for u in (-1, 0, 1)])
        await_recv(vertical[2])
        far += give_left_square([(0, 2)])
        mid += give_right_square([(u, 0) for u in (-1, 0, 1)])
        await_recv(vertical[1])
        for n, p in enumerate((1, -1)):
            give_tip[unit(n)] = product_tip(p).astype(jnp.bfloat16)
        tips = send_rows(give_tip, 0, tip_below, 0, 1, True, 13)
        tips += send_rows(give_tip, 1, tip_above, 0, 1, False, 13)
        near = []
        for u in (0, -1, 1):
            near += give_left_square([(u, 1)])
            near += give_right_square([(u, -1)])
        pass_on()
        for n, v in enumerate((-1, 1)):
            for u in (-1, 0, 1):
                acc[unit(n * 3 + u + 1)] = product_square(0, (u, v))
        await_recv(far, mid)
        finish_square((0, -2), None)
        finish_square((0, 2), None)
        for u in (-1, 0, 1):
            finish_square((u, 0), product_square(0, (u, 0)))
        sides = send(filtered.at[unit(0, 2)], side_right.at[unit(0, 2)], left)
        sides += send(filtered.at[unit(1, 2)], side_left.at[unit(0, 2)], right)
        await_recv(near)
        for u in (0, -1, 1):
            for n, v in enumerate((-1, 1)):
                finish_square((u, v), acc[unit(n * 3 + u + 1)])
            if u == 0:
                sides += send(filtered.at[unit(3)], side_right.at[unit(2)], left)
                sides += send(filtered.at[unit(4)], side_left.at[unit(2)], right)
        f_near = send_filtered(up_units[0:3], down_units[0:3])
        await_recv(tips)
        for u, tip in ((-2, tip_above), (2, tip_below)):
            finish_square((u, 0), tip[...].astype(jnp.float32))
        f_tip = send_filtered([(-2, 0)], [(2, 0)])
        pass_on()
        await_recv(sides)
        for n, p in enumerate((1, -1)):
            for v in (-1, 0, 1):
                give_rim[unit(n * 3 + v + 1)] = product_rim(p, v).astype(jnp.bfloat16)
        rims = send_rows(give_rim, 0, rim_below, 0, 3, True, 14)
        rims += send_rows(give_rim, 3, rim_above, 0, 3, False, 14)
        pass_on()
        pass_on()

        def give_left_cube(targets):
            return give(product_cube, 1, left_cube, targets, give_left2, got_right2, left)

        def give_right_cube(targets):
            return give(product_cube, -1, right_cube, targets, give_right2, got_left2, right)

        def finish_cube(t, total):
            u, v = t
            if t in left_cube:
                total = total + got_right2[unit(left_cube.index(t))].astype(jnp.float32)
            if t in right_cube:
                total = total + got_left2[unit(right_cube.index(t))].astype(jnp.float32)
            if u != 0:
                rim = rim_below if u == 1 else rim_above
                total = total + rim[unit(v + 1)].astype(jnp.float32)
            total = 1.5 * own[unit(given_at(u, v))].astype(jnp.float32) - 0.5 * total
            for l in range(2):
                for m in range(2):
                    keep = mask_x[0, 0, l, ((u + 1) * 3 + v + 1) * 2 + m] > 0
                    value = total[l * BS : (l + 1) * BS, m * BS : (m + 1) * BS]
                    out[l, u + 1, v + 1, m] = jnp.where(keep, value, jnp.zeros_like(value)).astype(
                        jnp.bfloat16
                    )

        c_parts = give_left_cube([(0, -1)]) + give_right_cube([(0, 1)])
        await_recv(f_near)
        line = [(u, 0) for u in (-1, 0, 1)]
        c_parts += give_left_cube(line) + give_right_cube(line)
        await_recv(f_tip)
        c_parts += give_left_cube([(u, 1) for u in (-1, 0, 1)])
        c_parts += give_right_cube([(u, -1) for u in (-1, 0, 1)])
        for v in (-1, 0, 1):
            for u in (-1, 0, 1):
                acc[unit((v + 1) * 3 + u + 1)] = product_cube(0, (u, v))
        await_recv(rims, c_parts)
        for v in (-1, 0, 1):
            for u in (-1, 0, 1):
                finish_cube((u, v), acc[unit((v + 1) * 3 + u + 1)])
        for copy in sent:
            copy.wait_send()
        for condition, _, onward in passed:

            @pl.when(condition)
            def _():
                onward.wait_send()


    return kernel


def solution(mesh):
    rows, cols = mesh.shape["row"], mesh.shape["col"]

    def units(n, dtype=jnp.bfloat16):
        return pltpu.VMEM((n * UNIT, UNIT), dtype)

    def local(values, mask_x, mask_sq):
        grid = values.reshape(2, 3, 3, 2, BS, BS)
        out = pl.pallas_call(
            make_kernel(rows, cols),
            out_shape=jax.ShapeDtypeStruct(grid.shape, jnp.bfloat16),
            in_specs=[
                pl.BlockSpec(memory_space=pltpu.HBM),
                pl.BlockSpec(memory_space=pltpu.HBM),
                pl.BlockSpec(memory_space=pltpu.HBM),
            ],
            out_specs=pl.BlockSpec(memory_space=pltpu.VMEM),
            scratch_shapes=[
                pltpu.SMEM(mask_x.shape, mask_x.dtype), pltpu.SMEM(mask_sq.shape, mask_sq.dtype),
                pltpu.VMEM((3, 2, 3, 2, BS, BS), jnp.bfloat16),
                units(9), units(9), units(9), units(3), units(3),
                units(7), units(7), units(7), units(7),
                units(13), units(4), units(4),
                units(7), units(7), units(7), units(7),
                units(17), units(2), units(1), units(1),
                units(3), units(3), units(6), units(3), units(3),
                units(9, jnp.float32),
                pltpu.SemaphoreType.DMA((5,)),
                pltpu.SemaphoreType.DMA((64,)),
                pltpu.SemaphoreType.DMA((64,)),
                pltpu.SemaphoreType.DMA((16,)),
                pltpu.SemaphoreType.DMA((16,)),
            ],
            compiler_params=pltpu.CompilerParams(
                collective_id=0, has_side_effects=True, vmem_limit_bytes=52 * 2**20
            ),
        )(grid, mask_x, mask_sq)
        return out.reshape(values.shape)

    return jax.shard_map(
        local,
        mesh=mesh,
        in_specs=(
            P("row", "col", None, None, None, None),
            P("row", "col", None, None),
            P("row", "col", None, None),
        ),
        out_specs=P("row", "col", None, None, None, None),
        check_vma=False,
    )
```

```python
import jax
import jax.numpy as jnp
from jax import lax
from jax.experimental import pallas as pl
from jax.experimental.pallas import tpu as pltpu
from jax.sharding import PartitionSpec as P

BS = 128
UNIT = 2 * BS
MESH = pl.DeviceIdType.MESH
X = 4
RUN = 8
AROUND = 8

up_units = [(-1, 0), (-1, -1), (-1, 1), (-2, 0)]
down_units = [(1, 0), (1, -1), (1, 1), (2, 0)]
square_units = [(0, -2), (0, 0), (0, 2), (0, -1), (0, 1)] + up_units + down_units
side_left_units = [(0, 0), (0, 2), (0, 1)]
side_right_units = [(0, -2), (0, 0), (0, -1)]
square_slots = [(u, v) for u in range(-2, 3) for v in range(-2, 3) if u * u + v * v <= 4]

left_square = [(u, 0) for u in (-1, 0, 1)] + [(0, 2)] + [(u, 1) for u in (-1, 0, 1)]
right_square = [(u, 0) for u in (-1, 0, 1)] + [(0, -2)] + [(u, -1) for u in (-1, 0, 1)]
left_cube = [(0, -1)] + [(u, v) for v in (0, 1) for u in (-1, 0, 1)]
right_cube = [(0, 1)] + [(u, v) for v in (0, -1) for u in (-1, 0, 1)]


def given_at(u, v):
    return (v + 1) * 3 + u + 1


def unit(n, count=1):
    return pl.ds(n * UNIT, count * UNIT)


def make_kernel(rows, cols):
    def kernel(
        values, mask_x_in, mask_sq_in, out,
        mask_x, mask_sq, staged, own, above, below, from_left, from_right,
        give_left, give_right, got_left, got_right,
        filtered, filt_above, filt_below,
        give_left2, give_right2, got_left2, got_right2,
        passing, give_tip, tip_above, tip_below, side_left, side_right, give_rim, rim_above, rim_below,
        passing_side, acc, load_sem, send_sem, recv_sem, pass_recv_sem, pass_send_sem, around_recv_sem, around_send_sem,
    ):
        a, b = lax.axis_index("row"), lax.axis_index("col")

        def row(shift):
            return (lax.rem(a + shift + rows, rows), b)

        up, down = row(-1), row(1)
        left = (a, lax.rem(b + cols - 1, cols))
        right = (a, lax.rem(b + 1, cols))
        x = lax.rem(a, X)
        first, last = x == 0, x == X - 1
        at_end = first | last
        run = lax.rem(b, RUN)
        wraps_left, wraps_right = run == 0, run == RUN - 1
        inward = jnp.where(x < X // 2, 1, -1)

        loads = {}
        for c in (0, 2, 1):
            loads[c] = pltpu.make_async_copy(values.at[:, :, c], staged.at[c], load_sem.at[c])
            loads[c].start()
        masks = [
            pltpu.make_async_copy(mask_x_in, mask_x, load_sem.at[3]),
            pltpu.make_async_copy(mask_sq_in, mask_sq, load_sem.at[4]),
        ]
        for copy in masks:
            copy.start()

        barrier = pltpu.get_barrier_semaphore()

        def greet(device):
            pl.semaphore_signal(barrier, inc=1, device_id=device, device_id_type=MESH)

        for device in (up, down, left, right):
            greet(device)

        @pl.when(first)
        def _():
            greet(row(X - 1))
            greet(row(-X))

        @pl.when(last)
        def _():
            greet(row(1 - X))
            greet(row(X))

        @pl.when(at_end & wraps_left)
        def _():
            greet((row(inward)[0], left[1]))

        @pl.when(at_end & wraps_right)
        def _():
            greet((row(inward)[0], right[1]))

        pl.semaphore_wait(barrier, jnp.where(at_end, 6, jnp.where(wraps_left | wraps_right, 5, 4)))

        sent = []

        def remote(src, dst, gone, come, device):
            return pltpu.make_async_remote_copy(
                src_ref=src, dst_ref=dst, send_sem=gone, recv_sem=come, device_id=device,
                device_id_type=MESH,
            )

        def make(src, dst, device):
            n = len(sent)
            copy = remote(src, dst, send_sem.at[n], recv_sem.at[n], device)
            sent.append(copy)
            return copy

        def send(src, dst, device):
            copy = make(src, dst, device)
            copy.start()
            return [copy]

        passed = []

        def send_rows(src, src_unit, dst, dst_unit, count, goes_up, base):
            device, at_wrap, partner = (up, first, row(X - 1)) if goes_up else (down, last, row(1 - X))
            half = count * UNIT // 2
            straight = make(
                src.at[pl.ds(src_unit * UNIT, half)], dst.at[pl.ds(dst_unit * UNIT, half)], device
            )
            n = len(passed) // 2
            src_half = src.at[pl.ds(src_unit * UNIT + half, half)]
            dst_half = dst.at[pl.ds(dst_unit * UNIT + half, half)]
            hold = passing.at[pl.ds((base + dst_unit) * UNIT + half, half)]
            other = make(src_half, dst_half, device)
            k = len(sent) - 1
            detour = pltpu.make_async_remote_copy(
                src_ref=src_half, dst_ref=hold, send_sem=send_sem.at[k],
                recv_sem=pass_recv_sem.at[n], device_id=partner, device_id_type=MESH,
            )
            onward = pltpu.make_async_remote_copy(
                src_ref=hold, dst_ref=dst_half, send_sem=pass_send_sem.at[n],
                recv_sem=recv_sem.at[k], device_id=row(-X if goes_up else X), device_id_type=MESH,
            )
            passed.append((last if goes_up else first, detour, onward))
            straight.start()

            @pl.when(at_wrap)
            def _():
                detour.start()

            @pl.when(jnp.logical_not(at_wrap))
            def _():
                other.start()

            return [straight, other]

        handed = [0]

        def pass_on():
            for condition, detour, onward in passed[handed[0] : handed[0] + 2]:

                @pl.when(condition)
                def _():
                    detour.wait_recv()
                    onward.start()

            handed[0] += 2

        side_relays = {True: [], False: []}

        def send_side(src, dst, at, count, goes_left, hold_at):
            size = count * UNIT
            lead = size - size * AROUND // 16
            device, at_wrap = (left, wraps_left) if goes_left else (right, wraps_right)

            def part(start, length):
                span = pl.ds(at * UNIT + start, length)
                return src.at[span], dst.at[span]

            plain = make(*part(0, size), device)
            n = len(sent) - 1
            gone, come = send_sem.at[n], recv_sem.at[n]
            straight = remote(*part(0, lead), gone, come, device)
            src_ref, dst_ref = part(lead, size - lead)
            hold = passing_side.at[pl.ds(hold_at * UNIT, size - lead)]
            k = len(side_relays[goes_left])
            there = remote(src_ref, hold, gone, around_recv_sem.at[k], row(inward))
            back = (lax.rem(a + rows - inward, rows), device[1])
            on = remote(hold, dst_ref, around_send_sem.at[k], come, back)
            side_relays[goes_left].append((there, on))

            @pl.when(at_wrap & at_end)
            def _():
                there.start()
                straight.start()

            @pl.when(jnp.logical_not(at_wrap & at_end))
            def _():
                plain.start()

            return [plain]

        def pass_around(start, stop):
            for goes_left, at_wrap in ((True, wraps_left), (False, wraps_right)):

                @pl.when(at_wrap & jnp.logical_not(at_end))
                def _():
                    for there, on in side_relays[goes_left][start:stop]:
                        there.wait_recv()
                        on.start()

        def blocks(ref, n):
            for l in range(2):
                for m in range(2):
                    yield l, m, ref.at[pl.ds(n * UNIT + l * BS, BS), pl.ds(m * BS, BS)]

        for copy in masks:
            copy.wait()

        def mask_column(c):
            loads[c].wait()
            for ui in range(3):
                for l, m, block in blocks(own, c * 3 + ui):
                    keep = mask_x[0, 0, l, (ui * 3 + c) * 2 + m] > 0
                    value = staged[c, l, ui, m]
                    block[...] = jnp.where(keep, value, jnp.zeros_like(value))

        mask_column(0)
        to_left = send(own.at[unit(0, 3)], from_right, left)
        mask_column(2)
        to_right = send(own.at[unit(6, 3)], from_left, right)
        vertical = {}
        for c in (0, 2, 1):
            if c == 1:
                mask_column(c)
            vertical[c] = send_rows(own, c * 3, below, c * 3, 2, True, 0)
            vertical[c] += send_rows(own, c * 3 + 1, above, c * 3 + 1, 2, False, 0)

        row_of = {-1: above, 0: own, 1: below}
        filt_of = {
            -1: (filt_above, down_units), 0: (filtered, square_units), 1: (filt_below, up_units)
        }
        factor = {
            1: lambda p: from_left[unit(p + 1)],
            -1: lambda p: from_right[unit(p + 1)],
            0: lambda p: own[unit(given_at(p, 0))],
        }

        def product_square(q, t):
            total = None
            for p in (-1, 0, 1):
                u, v = t[0] - p, t[1] - q
                if abs(u) <= 1 and abs(v) <= 1:
                    term = jnp.dot(
                        factor[q](p), row_of[p][unit(given_at(u, v))],
                        preferred_element_type=jnp.float32,
                    )
                    total = term if total is None else total + term
            return total

        def product_tip(p):
            total = None
            for q in (-1, 0, 1):
                right_factor = (from_left, own, from_right)[q + 1]
                at = given_at(p, 0) if q == 0 else p + 1
                term = jnp.dot(
                    (below, above)[(p + 1) // 2][unit(given_at(p, q))], right_factor[unit(at)],
                    preferred_element_type=jnp.float32,
                )
                total = term if total is None else total + term
            return total

        def product_cube(q, t):
            total = None
            for p in (-1, 0, 1):
                u, v = t[0] - p, t[1] - q
                if u * u + v * v <= 4 and (p == 0 or u != 0):
                    ref, order = filt_of[p]
                    term = jnp.dot(
                        factor[q](p), ref[unit(order.index((u, v)))],
                        preferred_element_type=jnp.float32,
                    )
                    total = term if total is None else total + term
            return total

        def product_rim(p, v):
            total = None
            for q in (-1, 0, 1):
                ref, order = (
                    (side_left, side_left_units), (filtered, square_units), (side_right, side_right_units)
                )[q + 1]
                term = jnp.dot(
                    (below, above)[(p + 1) // 2][unit(given_at(p, q))], ref[unit(order.index((0, v - q)))],
                    preferred_element_type=jnp.float32,
                )
                total = term if total is None else total + term
            return total

        def give(product, q, order, targets, buffer, landing, device, hold_at=None):
            at = order.index(targets[0])
            for n, t in enumerate(targets):
                buffer[unit(at + n)] = product(q, t).astype(jnp.bfloat16)
            if hold_at is not None:
                return send_side(buffer, landing, at, len(targets), q == 1, hold_at)
            span = unit(at, len(targets))
            return send(buffer.at[span], landing.at[span], device)

        def give_left_square(targets, hold_at=None):
            return give(product_square, 1, left_square, targets, give_left, got_right, left, hold_at)

        def give_right_square(targets, hold_at=None):
            return give(product_square, -1, right_square, targets, give_right, got_left, right, hold_at)

        def finish_square(t, total):
            if t in left_square:
                part = got_right[unit(left_square.index(t))].astype(jnp.float32)
                total = part if total is None else total + part
            if t in right_square:
                part = got_left[unit(right_square.index(t))].astype(jnp.float32)
                total = part if total is None else total + part
            total = total * (0.25 / BS)
            for l, m, block in blocks(filtered, square_units.index(t)):
                keep = mask_sq[0, 0, l, square_slots.index(t) * 2 + m] > 0
                value = total[l * BS : (l + 1) * BS, m * BS : (m + 1) * BS]
                block[...] = jnp.where(keep, value, jnp.zeros_like(value)).astype(jnp.bfloat16)

        def send_filtered(units_up, units_down):
            copies = []
            for units, order, landing, goes_up in (
                (units_up, up_units, filt_below, True), (units_down, down_units, filt_above, False)
            ):
                copies += send_rows(
                    filtered, square_units.index(units[0]), landing, order.index(units[0]),
                    len(units), goes_up, 9,
                )
            return copies

        def await_recv(*groups):
            for group in groups:
                for copy in group:
                    copy.wait_recv()

        def give_left_cube(targets, hold_at=None):
            return give(product_cube, 1, left_cube, targets, give_left2, got_right2, left, hold_at)

        def give_right_cube(targets, hold_at=None):
            return give(product_cube, -1, right_cube, targets, give_right2, got_left2, right, hold_at)

        pass_on()
        pass_on()
        pass_on()
        await_recv(to_left, to_right)
        await_recv(vertical[0])
        far = give_right_square([(0, -2)])
        mid = give_left_square([(u, 0) for u in (-1, 0, 1)], 0)
        await_recv(vertical[2])
        far += give_left_square([(0, 2)])
        mid += give_right_square([(u, 0) for u in (-1, 0, 1)], 0)
        await_recv(vertical[1])
        for n, p in enumerate((1, -1)):
            give_tip[unit(n)] = product_tip(p).astype(jnp.bfloat16)
        tips = send_rows(give_tip, 0, tip_below, 0, 1, True, 13)
        tips += send_rows(give_tip, 1, tip_above, 0, 1, False, 13)
        near = []
        for u in (0, -1, 1):
            near += give_left_square([(u, 1)], 4 + u)
            near += give_right_square([(u, -1)], 4 + u)
        for n, v in enumerate((-1, 1)):
            for u in (-1, 0, 1):
                acc[unit(n * 3 + u + 1)] = product_square(0, (u, v))
        pass_around(0, 1)
        await_recv(far, mid)
        finish_square((0, -2), None)
        finish_square((0, 2), None)
        for u in (-1, 0, 1):
            finish_square((u, 0), product_square(0, (u, 0)))
        sides = send(filtered.at[unit(0, 2)], side_right.at[unit(0, 2)], left)
        sides += send(filtered.at[unit(1, 2)], side_left.at[unit(0, 2)], right)
        pass_on()
        pass_around(1, 4)
        await_recv(near)
        for u in (0, -1, 1):
            for n, v in enumerate((-1, 1)):
                finish_square((u, v), acc[unit(n * 3 + u + 1)])
            if u == 0:
                sides += send(filtered.at[unit(3)], side_right.at[unit(2)], left)
                sides += send(filtered.at[unit(4)], side_left.at[unit(2)], right)
        f_near = send_filtered(up_units[0:3], down_units[0:3])
        await_recv(tips)
        for u, tip in ((-2, tip_above), (2, tip_below)):
            finish_square((u, 0), tip[...].astype(jnp.float32))
        f_tip = send_filtered([(-2, 0)], [(2, 0)])
        c_parts = give_left_cube([(0, -1)]) + give_right_cube([(0, 1)])
        pass_on()
        pass_on()
        await_recv(sides)
        for n, p in enumerate((1, -1)):
            for v in (-1, 0, 1):
                give_rim[unit(n * 3 + v + 1)] = product_rim(p, v).astype(jnp.bfloat16)
        rims = send_rows(give_rim, 0, rim_below, 0, 3, True, 14)
        rims += send_rows(give_rim, 3, rim_above, 0, 3, False, 14)

        def finish_cube(t, total):
            u, v = t
            if t in left_cube:
                total = total + got_right2[unit(left_cube.index(t))].astype(jnp.float32)
            if t in right_cube:
                total = total + got_left2[unit(right_cube.index(t))].astype(jnp.float32)
            if u != 0:
                rim = rim_below if u == 1 else rim_above
                total = total + rim[unit(v + 1)].astype(jnp.float32)
            total = 1.5 * own[unit(given_at(u, v))].astype(jnp.float32) - 0.5 * total
            for l in range(2):
                for m in range(2):
                    keep = mask_x[0, 0, l, ((u + 1) * 3 + v + 1) * 2 + m] > 0
                    value = total[l * BS : (l + 1) * BS, m * BS : (m + 1) * BS]
                    out[l, u + 1, v + 1, m] = jnp.where(keep, value, jnp.zeros_like(value)).astype(
                        jnp.bfloat16
                    )

        await_recv(f_near)
        line = [(u, 0) for u in (-1, 0, 1)]
        c_parts += give_left_cube(line, 6) + give_right_cube(line, 6)
        pass_on()
        await_recv(f_tip)
        c_parts += give_left_cube([(u, 1) for u in (-1, 0, 1)], 9)
        c_parts += give_right_cube([(u, -1) for u in (-1, 0, 1)], 9)
        pass_around(4, 6)
        for v in (-1, 0, 1):
            for u in (-1, 0, 1):
                acc[unit((v + 1) * 3 + u + 1)] = product_cube(0, (u, v))
        await_recv(rims, c_parts)
        for v in (-1, 0, 1):
            for u in (-1, 0, 1):
                finish_cube((u, v), acc[unit((v + 1) * 3 + u + 1)])
        for copy in sent:
            copy.wait_send()
        for goes_left, at_wrap in ((True, wraps_left), (False, wraps_right)):

            @pl.when(at_wrap & jnp.logical_not(at_end))
            def _():
                for _, on in side_relays[goes_left]:
                    on.wait_send()

        for condition, _, onward in passed:

            @pl.when(condition)
            def _():
                onward.wait_send()


    return kernel


def solution(mesh):
    rows, cols = mesh.shape["row"], mesh.shape["col"]

    def units(n, dtype=jnp.bfloat16):
        return pltpu.VMEM((n * UNIT, UNIT), dtype)

    def local(values, mask_x, mask_sq):
        grid = values.reshape(2, 3, 3, 2, BS, BS)
        out = pl.pallas_call(
            make_kernel(rows, cols),
            out_shape=jax.ShapeDtypeStruct(grid.shape, jnp.bfloat16),
            in_specs=[
                pl.BlockSpec(memory_space=pltpu.HBM),
                pl.BlockSpec(memory_space=pltpu.HBM),
                pl.BlockSpec(memory_space=pltpu.HBM),
            ],
            out_specs=pl.BlockSpec(memory_space=pltpu.VMEM),
            scratch_shapes=[
                pltpu.SMEM(mask_x.shape, mask_x.dtype), pltpu.SMEM(mask_sq.shape, mask_sq.dtype),
                pltpu.VMEM((3, 2, 3, 2, BS, BS), jnp.bfloat16),
                units(9), units(9), units(9), units(3), units(3),
                units(7), units(7), units(7), units(7),
                units(13), units(4), units(4),
                units(7), units(7), units(7), units(7),
                units(17), units(2), units(1), units(1),
                units(3), units(3), units(6), units(3), units(3),
                units(12), units(9, jnp.float32),
                pltpu.SemaphoreType.DMA((5,)),
                pltpu.SemaphoreType.DMA((64,)),
                pltpu.SemaphoreType.DMA((64,)),
                pltpu.SemaphoreType.DMA((16,)),
                pltpu.SemaphoreType.DMA((16,)),
                pltpu.SemaphoreType.DMA((6,)),
                pltpu.SemaphoreType.DMA((6,)),
            ],
            compiler_params=pltpu.CompilerParams(
                collective_id=0, has_side_effects=True, vmem_limit_bytes=52 * 2**20
            ),
        )(grid, mask_x, mask_sq)
        return out.reshape(values.shape)

    return jax.shard_map(
        local,
        mesh=mesh,
        in_specs=(
            P("row", "col", None, None, None, None),
            P("row", "col", None, None),
            P("row", "col", None, None),
        ),
        out_specs=P("row", "col", None, None, None, None),
        check_vma=False,
    )
```

```python
import jax
import jax.numpy as jnp
from jax import lax
from jax.experimental import pallas as pl
from jax.experimental.pallas import tpu as pltpu
from jax.sharding import PartitionSpec as P

BS = 128
UNIT = 2 * BS
MESH = pl.DeviceIdType.MESH
X = 4
RUN = 8
AROUND = 8

up_units = [(-1, 0), (-1, -1), (-1, 1), (-2, 0)]
down_units = [(1, 0), (1, -1), (1, 1), (2, 0)]
square_units = [(0, -2), (0, 0), (0, 2), (0, -1), (0, 1)] + up_units + down_units
side_left_units = [(0, 0), (0, 2), (0, 1)]
side_right_units = [(0, -2), (0, 0), (0, -1)]
square_slots = [(u, v) for u in range(-2, 3) for v in range(-2, 3) if u * u + v * v <= 4]

left_square = [(u, 0) for u in (-1, 0, 1)] + [(0, 2)] + [(u, 1) for u in (-1, 0, 1)]
right_square = [(u, 0) for u in (-1, 0, 1)] + [(0, -2)] + [(u, -1) for u in (-1, 0, 1)]
left_cube = [(0, -1)] + [(u, v) for v in (0, 1) for u in (-1, 0, 1)]
right_cube = [(0, 1)] + [(u, v) for v in (0, -1) for u in (-1, 0, 1)]


def given_at(u, v):
    return (v + 1) * 3 + u + 1


def unit(n, count=1):
    return pl.ds(n * UNIT, count * UNIT)


def make_kernel(rows, cols):
    def kernel(
        values, mask_x_in, mask_sq_in, out,
        mask_x, mask_sq, staged, own, above, below, from_left, from_right,
        give_left, give_right, got_left, got_right,
        filtered, filt_above, filt_below,
        give_left2, give_right2, got_left2, got_right2,
        passing, give_tip, tip_above, tip_below, side_left, side_right, give_rim, rim_above, rim_below,
        passing_side, acc, load_sem, send_sem, recv_sem, pass_recv_sem, pass_send_sem, around_recv_sem, around_send_sem,
    ):
        a, b = lax.axis_index("row"), lax.axis_index("col")

        def row(shift):
            return (lax.rem(a + shift + rows, rows), b)

        up, down = row(-1), row(1)
        left = (a, lax.rem(b + cols - 1, cols))
        right = (a, lax.rem(b + 1, cols))
        x = lax.rem(a, X)
        first, last = x == 0, x == X - 1
        at_end = first | last
        run = lax.rem(b, RUN)
        wraps_left, wraps_right = run == 0, run == RUN - 1
        inward = jnp.where(x < X // 2, 1, -1)

        loads = {}
        for c in (0, 2, 1):
            loads[c] = pltpu.make_async_copy(values.at[:, :, c], staged.at[c], load_sem.at[c])
            loads[c].start()
        masks = [
            pltpu.make_async_copy(mask_x_in, mask_x, load_sem.at[3]),
            pltpu.make_async_copy(mask_sq_in, mask_sq, load_sem.at[4]),
        ]
        for copy in masks:
            copy.start()

        barrier = pltpu.get_barrier_semaphore()

        def greet(device):
            pl.semaphore_signal(barrier, inc=1, device_id=device, device_id_type=MESH)

        for device in (up, down, left, right):
            greet(device)

        @pl.when(first)
        def _():
            greet(row(X - 1))
            greet(row(-X))

        @pl.when(last)
        def _():
            greet(row(1 - X))
            greet(row(X))

        @pl.when(at_end & wraps_left)
        def _():
            greet((row(inward)[0], left[1]))

        @pl.when(at_end & wraps_right)
        def _():
            greet((row(inward)[0], right[1]))

        pl.semaphore_wait(barrier, jnp.where(at_end, 6, jnp.where(wraps_left | wraps_right, 5, 4)))

        sent = []

        def remote(src, dst, gone, come, device):
            return pltpu.make_async_remote_copy(
                src_ref=src, dst_ref=dst, send_sem=gone, recv_sem=come, device_id=device,
                device_id_type=MESH,
            )

        def make(src, dst, device):
            n = len(sent)
            copy = remote(src, dst, send_sem.at[n], recv_sem.at[n], device)
            sent.append(copy)
            return copy

        def send(src, dst, device):
            copy = make(src, dst, device)
            copy.start()
            return [copy]

        passed = []

        def send_rows(src, src_unit, dst, dst_unit, count, goes_up, base):
            device, at_wrap, partner = (up, first, row(X - 1)) if goes_up else (down, last, row(1 - X))
            half = count * UNIT // 2
            straight = make(
                src.at[pl.ds(src_unit * UNIT, half)], dst.at[pl.ds(dst_unit * UNIT, half)], device
            )
            n = len(passed) // 2
            src_half = src.at[pl.ds(src_unit * UNIT + half, half)]
            dst_half = dst.at[pl.ds(dst_unit * UNIT + half, half)]
            hold = passing.at[pl.ds((base + dst_unit) * UNIT + half, half)]
            other = make(src_half, dst_half, device)
            k = len(sent) - 1
            detour = pltpu.make_async_remote_copy(
                src_ref=src_half, dst_ref=hold, send_sem=send_sem.at[k],
                recv_sem=pass_recv_sem.at[n], device_id=partner, device_id_type=MESH,
            )
            onward = pltpu.make_async_remote_copy(
                src_ref=hold, dst_ref=dst_half, send_sem=pass_send_sem.at[n],
                recv_sem=recv_sem.at[k], device_id=row(-X if goes_up else X), device_id_type=MESH,
            )
            passed.append((last if goes_up else first, detour, onward))
            straight.start()

            @pl.when(at_wrap)
            def _():
                detour.start()

            @pl.when(jnp.logical_not(at_wrap))
            def _():
                other.start()

            return [straight, other]

        handed = [0]

        def pass_on():
            for condition, detour, onward in passed[handed[0] : handed[0] + 2]:

                @pl.when(condition)
                def _():
                    detour.wait_recv()
                    onward.start()

            handed[0] += 2

        side_relays = {True: [], False: []}

        def send_side(src, dst, at, count, goes_left, hold_at):
            size = count * UNIT
            lead = size - size * AROUND // 16
            device, at_wrap = (left, wraps_left) if goes_left else (right, wraps_right)

            def part(start, length):
                span = pl.ds(at * UNIT + start, length)
                return src.at[span], dst.at[span]

            plain = make(*part(0, size), device)
            n = len(sent) - 1
            gone, come = send_sem.at[n], recv_sem.at[n]
            straight = remote(*part(0, lead), gone, come, device)
            src_ref, dst_ref = part(lead, size - lead)
            hold = passing_side.at[pl.ds(hold_at * UNIT, size - lead)]
            k = len(side_relays[goes_left])
            there = remote(src_ref, hold, gone, around_recv_sem.at[k], row(inward))
            back = (lax.rem(a + rows - inward, rows), device[1])
            on = remote(hold, dst_ref, around_send_sem.at[k], come, back)
            side_relays[goes_left].append((there, on))

            @pl.when(at_wrap & at_end)
            def _():
                there.start()
                straight.start()

            @pl.when(jnp.logical_not(at_wrap & at_end))
            def _():
                plain.start()

            return [plain]

        def pass_around(start, stop):
            for goes_left, at_wrap in ((True, wraps_left), (False, wraps_right)):

                @pl.when(at_wrap & jnp.logical_not(at_end))
                def _():
                    for there, on in side_relays[goes_left][start:stop]:
                        there.wait_recv()
                        on.start()

        def blocks(ref, n):
            for l in range(2):
                for m in range(2):
                    yield l, m, ref.at[pl.ds(n * UNIT + l * BS, BS), pl.ds(m * BS, BS)]

        for copy in masks:
            copy.wait()

        def mask_column(c):
            loads[c].wait()
            for ui in range(3):
                for l, m, block in blocks(own, c * 3 + ui):
                    keep = mask_x[0, 0, l, (ui * 3 + c) * 2 + m] > 0
                    value = staged[c, l, ui, m]
                    block[...] = jnp.where(keep, value, jnp.zeros_like(value))

        mask_column(0)
        to_left = send(own.at[unit(0, 3)], from_right, left)
        mask_column(2)
        to_right = send(own.at[unit(6, 3)], from_left, right)
        vertical = {}
        for c in (0, 2, 1):
            if c == 1:
                mask_column(c)
            vertical[c] = send_rows(own, c * 3, below, c * 3, 2, True, 0)
            vertical[c] += send_rows(own, c * 3 + 1, above, c * 3 + 1, 2, False, 0)

        row_of = {-1: above, 0: own, 1: below}
        filt_of = {
            -1: (filt_above, down_units), 0: (filtered, square_units), 1: (filt_below, up_units)
        }
        factor = {
            1: lambda p: from_left[unit(p + 1)],
            -1: lambda p: from_right[unit(p + 1)],
            0: lambda p: own[unit(given_at(p, 0))],
        }

        def product_square(q, t):
            total = None
            for p in (-1, 0, 1):
                u, v = t[0] - p, t[1] - q
                if abs(u) <= 1 and abs(v) <= 1:
                    term = jnp.dot(
                        factor[q](p), row_of[p][unit(given_at(u, v))],
                        preferred_element_type=jnp.float32,
                    )
                    total = term if total is None else total + term
            return total

        def product_tip(p):
            total = None
            for q in (-1, 0, 1):
                right_factor = (from_left, own, from_right)[q + 1]
                at = given_at(p, 0) if q == 0 else p + 1
                term = jnp.dot(
                    (below, above)[(p + 1) // 2][unit(given_at(p, q))], right_factor[unit(at)],
                    preferred_element_type=jnp.float32,
                )
                total = term if total is None else total + term
            return total

        def product_cube(q, t):
            total = None
            for p in (-1, 0, 1):
                u, v = t[0] - p, t[1] - q
                if u * u + v * v <= 4 and (p == 0 or u != 0):
                    ref, order = filt_of[p]
                    term = jnp.dot(
                        factor[q](p), ref[unit(order.index((u, v)))],
                        preferred_element_type=jnp.float32,
                    )
                    total = term if total is None else total + term
            return total

        def product_rim(p, v):
            total = None
            for q in (-1, 0, 1):
                ref, order = (
                    (side_left, side_left_units), (filtered, square_units), (side_right, side_right_units)
                )[q + 1]
                term = jnp.dot(
                    (below, above)[(p + 1) // 2][unit(given_at(p, q))], ref[unit(order.index((0, v - q)))],
                    preferred_element_type=jnp.float32,
                )
                total = term if total is None else total + term
            return total

        def give(product, q, order, targets, buffer, landing, device, hold_at=None):
            at = order.index(targets[0])
            for n, t in enumerate(targets):
                buffer[unit(at + n)] = product(q, t).astype(jnp.bfloat16)
            if hold_at is not None:
                return send_side(buffer, landing, at, len(targets), q == 1, hold_at)
            span = unit(at, len(targets))
            return send(buffer.at[span], landing.at[span], device)

        def give_left_square(targets, hold_at=None):
            return give(product_square, 1, left_square, targets, give_left, got_right, left, hold_at)

        def give_right_square(targets, hold_at=None):
            return give(product_square, -1, right_square, targets, give_right, got_left, right, hold_at)

        def finish_square(t, total):
            if t in left_square:
                part = got_right[unit(left_square.index(t))].astype(jnp.float32)
                total = part if total is None else total + part
            if t in right_square:
                part = got_left[unit(right_square.index(t))].astype(jnp.float32)
                total = part if total is None else total + part
            total = total * (0.25 / BS)
            for l, m, block in blocks(filtered, square_units.index(t)):
                keep = mask_sq[0, 0, l, square_slots.index(t) * 2 + m] > 0
                value = total[l * BS : (l + 1) * BS, m * BS : (m + 1) * BS]
                block[...] = jnp.where(keep, value, jnp.zeros_like(value)).astype(jnp.bfloat16)

        def send_filtered(units_up, units_down):
            copies = []
            for units, order, landing, goes_up in (
                (units_up, up_units, filt_below, True), (units_down, down_units, filt_above, False)
            ):
                copies += send_rows(
                    filtered, square_units.index(units[0]), landing, order.index(units[0]),
                    len(units), goes_up, 9,
                )
            return copies

        def await_recv(*groups):
            for group in groups:
                for copy in group:
                    copy.wait_recv()

        def give_left_cube(targets, hold_at=None):
            return give(product_cube, 1, left_cube, targets, give_left2, got_right2, left, hold_at)

        def give_right_cube(targets, hold_at=None):
            return give(product_cube, -1, right_cube, targets, give_right2, got_left2, right, hold_at)

        pass_on()
        pass_on()
        pass_on()
        await_recv(to_left, to_right)
        await_recv(vertical[0])
        far = give_right_square([(0, -2)])
        mid = give_left_square([(u, 0) for u in (-1, 0, 1)], 0)
        await_recv(vertical[2])
        far += give_left_square([(0, 2)])
        mid += give_right_square([(u, 0) for u in (-1, 0, 1)], 0)
        await_recv(vertical[1])
        for n, p in enumerate((1, -1)):
            give_tip[unit(n)] = product_tip(p).astype(jnp.bfloat16)
        tips = send_rows(give_tip, 0, tip_below, 0, 1, True, 13)
        tips += send_rows(give_tip, 1, tip_above, 0, 1, False, 13)
        near = []
        for u in (0, -1, 1):
            near += give_left_square([(u, 1)], 4 + u)
            near += give_right_square([(u, -1)], 4 + u)
        for n, v in enumerate((-1, 1)):
            for u in (-1, 0, 1):
                acc[unit(n * 3 + u + 1)] = product_square(0, (u, v))
        pass_around(0, 1)
        await_recv(far, mid)
        finish_square((0, -2), None)
        finish_square((0, 2), None)
        for u in (-1, 0, 1):
            finish_square((u, 0), product_square(0, (u, 0)))
        sides = send(filtered.at[unit(0, 2)], side_right.at[unit(0, 2)], left)
        sides += send(filtered.at[unit(1, 2)], side_left.at[unit(0, 2)], right)
        pass_on()
        pass_around(1, 4)
        await_recv(near)
        for u in (0, -1, 1):
            for n, v in enumerate((-1, 1)):
                finish_square((u, v), acc[unit(n * 3 + u + 1)])
            if u == 0:
                sides += send(filtered.at[unit(3)], side_right.at[unit(2)], left)
                sides += send(filtered.at[unit(4)], side_left.at[unit(2)], right)
        f_near = send_filtered(up_units[0:3], down_units[0:3])
        await_recv(tips)
        for u, tip in ((-2, tip_above), (2, tip_below)):
            finish_square((u, 0), tip[...].astype(jnp.float32))
        f_tip = send_filtered([(-2, 0)], [(2, 0)])
        c_parts = give_left_cube([(0, -1)]) + give_right_cube([(0, 1)])
        pass_on()
        pass_on()
        await_recv(sides)
        for n, p in enumerate((1, -1)):
            for v in (-1, 0, 1):
                give_rim[unit(n * 3 + v + 1)] = product_rim(p, v).astype(jnp.bfloat16)
        rims = send_rows(give_rim, 0, rim_below, 0, 3, True, 14)
        rims += send_rows(give_rim, 3, rim_above, 0, 3, False, 14)

        def finish_cube(t, total):
            u, v = t
            if t in left_cube:
                total = total + got_right2[unit(left_cube.index(t))].astype(jnp.float32)
            if t in right_cube:
                total = total + got_left2[unit(right_cube.index(t))].astype(jnp.float32)
            if u != 0:
                rim = rim_below if u == 1 else rim_above
                total = total + rim[unit(v + 1)].astype(jnp.float32)
            total = 1.5 * own[unit(given_at(u, v))].astype(jnp.float32) - 0.5 * total
            for l in range(2):
                for m in range(2):
                    keep = mask_x[0, 0, l, ((u + 1) * 3 + v + 1) * 2 + m] > 0
                    value = total[l * BS : (l + 1) * BS, m * BS : (m + 1) * BS]
                    out[l, u + 1, v + 1, m] = jnp.where(keep, value, jnp.zeros_like(value)).astype(
                        jnp.bfloat16
                    )

        await_recv(f_near)
        for u in (-1, 0, 1):
            c_parts += give_left_cube([(u, 0)], 7 + u) + give_right_cube([(u, 0)], 7 + u)
        pass_on()
        await_recv(f_tip)
        for u in (-1, 0, 1):
            c_parts += give_left_cube([(u, 1)], 10 + u) + give_right_cube([(u, -1)], 10 + u)
        pass_around(4, 10)
        for v in (-1, 0, 1):
            for u in (-1, 0, 1):
                acc[unit((v + 1) * 3 + u + 1)] = product_cube(0, (u, v))
        await_recv(rims, c_parts)
        for v in (-1, 0, 1):
            for u in (-1, 0, 1):
                finish_cube((u, v), acc[unit((v + 1) * 3 + u + 1)])
        for copy in sent:
            copy.wait_send()
        for goes_left, at_wrap in ((True, wraps_left), (False, wraps_right)):

            @pl.when(at_wrap & jnp.logical_not(at_end))
            def _():
                for _, on in side_relays[goes_left]:
                    on.wait_send()

        for condition, _, onward in passed:

            @pl.when(condition)
            def _():
                onward.wait_send()


    return kernel


def solution(mesh):
    rows, cols = mesh.shape["row"], mesh.shape["col"]

    def units(n, dtype=jnp.bfloat16):
        return pltpu.VMEM((n * UNIT, UNIT), dtype)

    def local(values, mask_x, mask_sq):
        grid = values.reshape(2, 3, 3, 2, BS, BS)
        out = pl.pallas_call(
            make_kernel(rows, cols),
            out_shape=jax.ShapeDtypeStruct(grid.shape, jnp.bfloat16),
            in_specs=[
                pl.BlockSpec(memory_space=pltpu.HBM),
                pl.BlockSpec(memory_space=pltpu.HBM),
                pl.BlockSpec(memory_space=pltpu.HBM),
            ],
            out_specs=pl.BlockSpec(memory_space=pltpu.VMEM),
            scratch_shapes=[
                pltpu.SMEM(mask_x.shape, mask_x.dtype), pltpu.SMEM(mask_sq.shape, mask_sq.dtype),
                pltpu.VMEM((3, 2, 3, 2, BS, BS), jnp.bfloat16),
                units(9), units(9), units(9), units(3), units(3),
                units(7), units(7), units(7), units(7),
                units(13), units(4), units(4),
                units(7), units(7), units(7), units(7),
                units(17), units(2), units(1), units(1),
                units(3), units(3), units(6), units(3), units(3),
                units(12), units(9, jnp.float32),
                pltpu.SemaphoreType.DMA((5,)),
                pltpu.SemaphoreType.DMA((64,)),
                pltpu.SemaphoreType.DMA((64,)),
                pltpu.SemaphoreType.DMA((16,)),
                pltpu.SemaphoreType.DMA((16,)),
                pltpu.SemaphoreType.DMA((10,)),
                pltpu.SemaphoreType.DMA((10,)),
            ],
            compiler_params=pltpu.CompilerParams(
                collective_id=0, has_side_effects=True, vmem_limit_bytes=52 * 2**20
            ),
        )(grid, mask_x, mask_sq)
        return out.reshape(values.shape)

    return jax.shard_map(
        local,
        mesh=mesh,
        in_specs=(
            P("row", "col", None, None, None, None),
            P("row", "col", None, None),
            P("row", "col", None, None),
        ),
        out_specs=P("row", "col", None, None, None, None),
        check_vma=False,
    )
```

```python
import jax
import jax.numpy as jnp
from jax import lax
from jax.experimental import pallas as pl
from jax.experimental.pallas import tpu as pltpu
from jax.sharding import PartitionSpec as P

BS = 128
UNIT = 2 * BS
MESH = pl.DeviceIdType.MESH
X = 4
RUN = 8
AROUND = 8

up_units = [(-1, 0), (-1, -1), (-1, 1), (-2, 0)]
down_units = [(1, 0), (1, -1), (1, 1), (2, 0)]
square_units = [(0, -2), (0, 0), (0, 2), (0, -1), (0, 1)] + up_units + down_units
side_left_units = [(0, 0), (0, 2), (0, 1)]
side_right_units = [(0, -2), (0, 0), (0, -1)]
square_slots = [(u, v) for u in range(-2, 3) for v in range(-2, 3) if u * u + v * v <= 4]

left_square = [(u, 0) for u in (-1, 0, 1)] + [(0, 2)] + [(u, 1) for u in (-1, 0, 1)]
right_square = [(u, 0) for u in (-1, 0, 1)] + [(0, -2)] + [(u, -1) for u in (-1, 0, 1)]
left_cube = [(0, -1)] + [(u, v) for v in (0, 1) for u in (-1, 0, 1)]
right_cube = [(0, 1)] + [(u, v) for v in (0, -1) for u in (-1, 0, 1)]


def given_at(u, v):
    return (v + 1) * 3 + u + 1


def unit(n, count=1):
    return pl.ds(n * UNIT, count * UNIT)


def make_kernel(rows, cols):
    def kernel(
        values, mask_x_in, mask_sq_in, out,
        mask_x, mask_sq, staged, own, above, below, from_left, from_right,
        give_left, give_right, got_left, got_right,
        filtered, filt_above, filt_below,
        give_left2, give_right2, got_left2, got_right2,
        passing, give_tip, tip_above, tip_below, side_left, side_right, give_rim, rim_above, rim_below,
        passing_side, acc, load_sem, send_sem, recv_sem, pass_recv_sem, pass_send_sem, around_recv_sem, around_send_sem,
    ):
        a, b = lax.axis_index("row"), lax.axis_index("col")

        def row(shift):
            return (lax.rem(a + shift + rows, rows), b)

        up, down = row(-1), row(1)
        left = (a, lax.rem(b + cols - 1, cols))
        right = (a, lax.rem(b + 1, cols))
        x = lax.rem(a, X)
        first, last = x == 0, x == X - 1
        at_end = first | last
        run = lax.rem(b, RUN)
        wraps_left, wraps_right = run == 0, run == RUN - 1
        inward = jnp.where(x < X // 2, 1, -1)

        loads = {}
        for c in (0, 2, 1):
            loads[c] = pltpu.make_async_copy(values.at[:, :, c], staged.at[c], load_sem.at[c])
            loads[c].start()
        masks = [
            pltpu.make_async_copy(mask_x_in, mask_x, load_sem.at[3]),
            pltpu.make_async_copy(mask_sq_in, mask_sq, load_sem.at[4]),
        ]
        for copy in masks:
            copy.start()

        barrier = pltpu.get_barrier_semaphore()

        def greet(device):
            pl.semaphore_signal(barrier, inc=1, device_id=device, device_id_type=MESH)

        for device in (up, down, left, right):
            greet(device)

        @pl.when(first)
        def _():
            greet(row(X - 1))
            greet(row(-X))

        @pl.when(last)
        def _():
            greet(row(1 - X))
            greet(row(X))

        @pl.when(at_end & wraps_left)
        def _():
            greet((row(inward)[0], left[1]))

        @pl.when(at_end & wraps_right)
        def _():
            greet((row(inward)[0], right[1]))

        pl.semaphore_wait(barrier, jnp.where(at_end, 6, jnp.where(wraps_left | wraps_right, 5, 4)))

        sent = []

        def remote(src, dst, gone, come, device):
            return pltpu.make_async_remote_copy(
                src_ref=src, dst_ref=dst, send_sem=gone, recv_sem=come, device_id=device,
                device_id_type=MESH,
            )

        def make(src, dst, device):
            n = len(sent)
            copy = remote(src, dst, send_sem.at[n], recv_sem.at[n], device)
            sent.append(copy)
            return copy

        def send(src, dst, device):
            copy = make(src, dst, device)
            copy.start()
            return [copy]

        passed = []

        def send_rows(src, src_unit, dst, dst_unit, count, goes_up, base):
            device, at_wrap, partner = (up, first, row(X - 1)) if goes_up else (down, last, row(1 - X))
            half = count * UNIT // 2
            straight = make(
                src.at[pl.ds(src_unit * UNIT, half)], dst.at[pl.ds(dst_unit * UNIT, half)], device
            )
            n = len(passed) // 2
            src_half = src.at[pl.ds(src_unit * UNIT + half, half)]
            dst_half = dst.at[pl.ds(dst_unit * UNIT + half, half)]
            hold = passing.at[pl.ds((base + dst_unit) * UNIT + half, half)]
            other = make(src_half, dst_half, device)
            k = len(sent) - 1
            detour = pltpu.make_async_remote_copy(
                src_ref=src_half, dst_ref=hold, send_sem=send_sem.at[k],
                recv_sem=pass_recv_sem.at[n], device_id=partner, device_id_type=MESH,
            )
            onward = pltpu.make_async_remote_copy(
                src_ref=hold, dst_ref=dst_half, send_sem=pass_send_sem.at[n],
                recv_sem=recv_sem.at[k], device_id=row(-X if goes_up else X), device_id_type=MESH,
            )
            passed.append((last if goes_up else first, detour, onward))
            straight.start()

            @pl.when(at_wrap)
            def _():
                detour.start()

            @pl.when(jnp.logical_not(at_wrap))
            def _():
                other.start()

            return [straight, other]

        handed = [0]

        def pass_on():
            for condition, detour, onward in passed[handed[0] : handed[0] + 2]:

                @pl.when(condition)
                def _():
                    detour.wait_recv()
                    onward.start()

            handed[0] += 2

        side_relays = {True: [], False: []}

        def send_side(src, dst, at, count, goes_left, hold_at):
            size = count * UNIT
            lead = size - size * AROUND // 16
            device, at_wrap = (left, wraps_left) if goes_left else (right, wraps_right)

            def part(start, length):
                span = pl.ds(at * UNIT + start, length)
                return src.at[span], dst.at[span]

            plain = make(*part(0, size), device)
            n = len(sent) - 1
            gone, come = send_sem.at[n], recv_sem.at[n]
            straight = remote(*part(0, lead), gone, come, device)
            src_ref, dst_ref = part(lead, size - lead)
            hold = passing_side.at[pl.ds(hold_at * UNIT, size - lead)]
            k = len(side_relays[goes_left])
            there = remote(src_ref, hold, gone, around_recv_sem.at[k], row(inward))
            back = (lax.rem(a + rows - inward, rows), device[1])
            on = remote(hold, dst_ref, around_send_sem.at[k], come, back)
            side_relays[goes_left].append((there, on))

            @pl.when(at_wrap & at_end)
            def _():
                there.start()
                straight.start()

            @pl.when(jnp.logical_not(at_wrap & at_end))
            def _():
                plain.start()

            return [plain]

        def pass_around(start, stop):
            for goes_left, at_wrap in ((True, wraps_left), (False, wraps_right)):

                @pl.when(at_wrap & jnp.logical_not(at_end))
                def _():
                    for there, on in side_relays[goes_left][start:stop]:
                        there.wait_recv()
                        on.start()

        def blocks(ref, n):
            for l in range(2):
                for m in range(2):
                    yield l, m, ref.at[pl.ds(n * UNIT + l * BS, BS), pl.ds(m * BS, BS)]

        for copy in masks:
            copy.wait()

        def mask_column(c):
            loads[c].wait()
            for ui in range(3):
                for l, m, block in blocks(own, c * 3 + ui):
                    keep = mask_x[0, 0, l, (ui * 3 + c) * 2 + m] > 0
                    value = staged[c, l, ui, m]
                    block[...] = jnp.where(keep, value, jnp.zeros_like(value))

        mask_column(0)
        to_left = send(own.at[unit(0, 3)], from_right, left)
        mask_column(2)
        to_right = send(own.at[unit(6, 3)], from_left, right)
        vertical = {}
        for c in (0, 2, 1):
            if c == 1:
                mask_column(c)
            vertical[c] = send_rows(own, c * 3, below, c * 3, 2, True, 0)
            vertical[c] += send_rows(own, c * 3 + 1, above, c * 3 + 1, 2, False, 0)

        row_of = {-1: above, 0: own, 1: below}
        filt_of = {
            -1: (filt_above, down_units), 0: (filtered, square_units), 1: (filt_below, up_units)
        }
        factor = {
            1: lambda p: from_left[unit(p + 1)],
            -1: lambda p: from_right[unit(p + 1)],
            0: lambda p: own[unit(given_at(p, 0))],
        }

        def product_square(q, t):
            total = None
            for p in (-1, 0, 1):
                u, v = t[0] - p, t[1] - q
                if abs(u) <= 1 and abs(v) <= 1:
                    term = jnp.dot(
                        factor[q](p), row_of[p][unit(given_at(u, v))],
                        preferred_element_type=jnp.float32,
                    )
                    total = term if total is None else total + term
            return total

        def product_tip(p):
            total = None
            for q in (-1, 0, 1):
                right_factor = (from_left, own, from_right)[q + 1]
                at = given_at(p, 0) if q == 0 else p + 1
                term = jnp.dot(
                    (below, above)[(p + 1) // 2][unit(given_at(p, q))], right_factor[unit(at)],
                    preferred_element_type=jnp.float32,
                )
                total = term if total is None else total + term
            return total

        def product_cube(q, t):
            total = None
            for p in (-1, 0, 1):
                u, v = t[0] - p, t[1] - q
                if u * u + v * v <= 4 and (p == 0 or u != 0):
                    ref, order = filt_of[p]
                    term = jnp.dot(
                        factor[q](p), ref[unit(order.index((u, v)))],
                        preferred_element_type=jnp.float32,
                    )
                    total = term if total is None else total + term
            return total

        def product_rim(p, v):
            total = None
            for q in (-1, 0, 1):
                ref, order = (
                    (side_left, side_left_units), (filtered, square_units), (side_right, side_right_units)
                )[q + 1]
                term = jnp.dot(
                    (below, above)[(p + 1) // 2][unit(given_at(p, q))], ref[unit(order.index((0, v - q)))],
                    preferred_element_type=jnp.float32,
                )
                total = term if total is None else total + term
            return total

        def give(product, q, order, targets, buffer, landing, device, hold_at=None):
            at = order.index(targets[0])
            for n, t in enumerate(targets):
                buffer[unit(at + n)] = product(q, t).astype(jnp.bfloat16)
            if hold_at is not None:
                return send_side(buffer, landing, at, len(targets), q == 1, hold_at)
            span = unit(at, len(targets))
            return send(buffer.at[span], landing.at[span], device)

        def give_left_square(targets, hold_at=None):
            return give(product_square, 1, left_square, targets, give_left, got_right, left, hold_at)

        def give_right_square(targets, hold_at=None):
            return give(product_square, -1, right_square, targets, give_right, got_left, right, hold_at)

        def finish_square(t, total):
            if t in left_square:
                part = got_right[unit(left_square.index(t))].astype(jnp.float32)
                total = part if total is None else total + part
            if t in right_square:
                part = got_left[unit(right_square.index(t))].astype(jnp.float32)
                total = part if total is None else total + part
            total = total * (0.25 / BS)
            for l, m, block in blocks(filtered, square_units.index(t)):
                keep = mask_sq[0, 0, l, square_slots.index(t) * 2 + m] > 0
                value = total[l * BS : (l + 1) * BS, m * BS : (m + 1) * BS]
                block[...] = jnp.where(keep, value, jnp.zeros_like(value)).astype(jnp.bfloat16)

        def send_filtered(units_up, units_down):
            copies = []
            for units, order, landing, goes_up in (
                (units_up, up_units, filt_below, True), (units_down, down_units, filt_above, False)
            ):
                copies += send_rows(
                    filtered, square_units.index(units[0]), landing, order.index(units[0]),
                    len(units), goes_up, 9,
                )
            return copies

        def await_recv(*groups):
            for group in groups:
                for copy in group:
                    copy.wait_recv()

        def give_left_cube(targets, hold_at=None):
            return give(product_cube, 1, left_cube, targets, give_left2, got_right2, left, hold_at)

        def give_right_cube(targets, hold_at=None):
            return give(product_cube, -1, right_cube, targets, give_right2, got_left2, right, hold_at)

        pass_on()
        pass_on()
        pass_on()
        await_recv(to_left, to_right)
        await_recv(vertical[0])
        far = give_right_square([(0, -2)])
        mid = give_left_square([(u, 0) for u in (-1, 0, 1)], 0)
        await_recv(vertical[2])
        far += give_left_square([(0, 2)])
        mid += give_right_square([(u, 0) for u in (-1, 0, 1)], 0)
        await_recv(vertical[1])
        for n, p in enumerate((1, -1)):
            give_tip[unit(n)] = product_tip(p).astype(jnp.bfloat16)
        tips = send_rows(give_tip, 0, tip_below, 0, 1, True, 13)
        tips += send_rows(give_tip, 1, tip_above, 0, 1, False, 13)
        near = []
        for u in (0, -1, 1):
            near += give_left_square([(u, 1)], 4 + u)
            near += give_right_square([(u, -1)], 4 + u)
        for n, v in enumerate((-1, 1)):
            for u in (-1, 0, 1):
                acc[unit(n * 3 + u + 1)] = product_square(0, (u, v))
        pass_around(0, 1)
        await_recv(far, mid)
        finish_square((0, -2), None)
        finish_square((0, 2), None)
        for u in (-1, 0, 1):
            finish_square((u, 0), product_square(0, (u, 0)))
        sides = send(filtered.at[unit(0, 2)], side_right.at[unit(0, 2)], left)
        sides += send(filtered.at[unit(1, 2)], side_left.at[unit(0, 2)], right)
        pass_on()
        pass_around(1, 4)
        await_recv(near)
        for u in (0, -1, 1):
            for n, v in enumerate((-1, 1)):
                finish_square((u, v), acc[unit(n * 3 + u + 1)])
            if u == 0:
                sides += send(filtered.at[unit(3)], side_right.at[unit(2)], left)
                sides += send(filtered.at[unit(4)], side_left.at[unit(2)], right)
        f_near = send_filtered(up_units[0:3], down_units[0:3])
        await_recv(tips)
        for u, tip in ((-2, tip_above), (2, tip_below)):
            finish_square((u, 0), tip[...].astype(jnp.float32))
        f_tip = send_filtered([(-2, 0)], [(2, 0)])
        c_parts = give_left_cube([(0, -1)]) + give_right_cube([(0, 1)])
        pass_on()
        pass_on()
        await_recv(sides)
        for n, p in enumerate((1, -1)):
            for v in (-1, 0, 1):
                give_rim[unit(n * 3 + v + 1)] = product_rim(p, v).astype(jnp.bfloat16)
        rims = send_rows(give_rim, 0, rim_below, 0, 3, True, 14)
        rims += send_rows(give_rim, 3, rim_above, 0, 3, False, 14)

        def finish_cube(t, total):
            u, v = t
            if t in left_cube:
                total = total + got_right2[unit(left_cube.index(t))].astype(jnp.float32)
            if t in right_cube:
                total = total + got_left2[unit(right_cube.index(t))].astype(jnp.float32)
            if u != 0:
                rim = rim_below if u == 1 else rim_above
                total = total + rim[unit(v + 1)].astype(jnp.float32)
            total = 1.5 * own[unit(given_at(u, v))].astype(jnp.float32) - 0.5 * total
            for l in range(2):
                for m in range(2):
                    keep = mask_x[0, 0, l, ((u + 1) * 3 + v + 1) * 2 + m] > 0
                    value = total[l * BS : (l + 1) * BS, m * BS : (m + 1) * BS]
                    out[l, u + 1, v + 1, m] = jnp.where(keep, value, jnp.zeros_like(value)).astype(
                        jnp.bfloat16
                    )

        await_recv(f_near)
        pass_on()
        for u in (-1, 0, 1):
            c_parts += give_left_cube([(u, 0)], 7 + u) + give_right_cube([(u, 0)], 7 + u)
        await_recv(f_tip)
        for u in (-1, 0, 1):
            c_parts += give_left_cube([(u, 1)], 10 + u) + give_right_cube([(u, -1)], 10 + u)
        pass_around(4, 10)
        for v in (-1, 0, 1):
            for u in (-1, 0, 1):
                acc[unit((v + 1) * 3 + u + 1)] = product_cube(0, (u, v))
        await_recv(rims, c_parts)
        for v in (-1, 0, 1):
            for u in (-1, 0, 1):
                finish_cube((u, v), acc[unit((v + 1) * 3 + u + 1)])
        for copy in sent:
            copy.wait_send()
        for goes_left, at_wrap in ((True, wraps_left), (False, wraps_right)):

            @pl.when(at_wrap & jnp.logical_not(at_end))
            def _():
                for _, on in side_relays[goes_left]:
                    on.wait_send()

        for condition, _, onward in passed:

            @pl.when(condition)
            def _():
                onward.wait_send()


    return kernel


def solution(mesh):
    rows, cols = mesh.shape["row"], mesh.shape["col"]

    def units(n, dtype=jnp.bfloat16):
        return pltpu.VMEM((n * UNIT, UNIT), dtype)

    def local(values, mask_x, mask_sq):
        grid = values.reshape(2, 3, 3, 2, BS, BS)
        out = pl.pallas_call(
            make_kernel(rows, cols),
            out_shape=jax.ShapeDtypeStruct(grid.shape, jnp.bfloat16),
            in_specs=[
                pl.BlockSpec(memory_space=pltpu.HBM),
                pl.BlockSpec(memory_space=pltpu.HBM),
                pl.BlockSpec(memory_space=pltpu.HBM),
            ],
            out_specs=pl.BlockSpec(memory_space=pltpu.VMEM),
            scratch_shapes=[
                pltpu.SMEM(mask_x.shape, mask_x.dtype), pltpu.SMEM(mask_sq.shape, mask_sq.dtype),
                pltpu.VMEM((3, 2, 3, 2, BS, BS), jnp.bfloat16),
                units(9), units(9), units(9), units(3), units(3),
                units(7), units(7), units(7), units(7),
                units(13), units(4), units(4),
                units(7), units(7), units(7), units(7),
                units(17), units(2), units(1), units(1),
                units(3), units(3), units(6), units(3), units(3),
                units(12), units(9, jnp.float32),
                pltpu.SemaphoreType.DMA((5,)),
                pltpu.SemaphoreType.DMA((64,)),
                pltpu.SemaphoreType.DMA((64,)),
                pltpu.SemaphoreType.DMA((16,)),
                pltpu.SemaphoreType.DMA((16,)),
                pltpu.SemaphoreType.DMA((10,)),
                pltpu.SemaphoreType.DMA((10,)),
            ],
            compiler_params=pltpu.CompilerParams(
                collective_id=0, has_side_effects=True, vmem_limit_bytes=52 * 2**20
            ),
        )(grid, mask_x, mask_sq)
        return out.reshape(values.shape)

    return jax.shard_map(
        local,
        mesh=mesh,
        in_specs=(
            P("row", "col", None, None, None, None),
            P("row", "col", None, None),
            P("row", "col", None, None),
        ),
        out_specs=P("row", "col", None, None, None, None),
        check_vma=False,
    )
```
